256 devices in a mesh: row: 16 (over y, z_hi), col: 16 (over x, z_lo, core).
Axes of the slice: x: 4, y: 4, z: 8 (z_hi: 4, z_lo: 2; z = z_hi * 2 + z_lo), core: 2. Of those that a mesh axis runs over, the one named last changes fastest.
Arguments:
- pair: bfloat16 [1024, 1024, 128], P('row', 'col'), may hold values from -6 to 6
- projection: bfloat16 [128, 640], replicated, may hold values from -0.5 to 0.5
- out_weight: bfloat16 [128, 128], replicated, may hold values from -0.5 to 0.5
Outputs:
- update: bfloat16 [1024, 1024, 128], P('row', 'col')
The draws below stay inside these ranges and needn't reach their ends.
All inputs are finite; a program needn't handle non-finite values.
Results may differ from the reference program's by a relative error of at most 0.013.
Values may be sent and summed in bfloat16 or wider, within the bound.
A program may use at most 128 MiB of HBM per device.

```python
import math
import jax
import jax.numpy as jnp
from jax import lax

C = 128
CH = 128
N = 1024


def steps_of(rng, extent, cuts, low, top_value):
    factor_of, own = 1.0, jax.random.fold_in(rng, 6)
    for position, shards_of in cuts:
        heights = jnp.exp(jax.random.uniform(jax.random.fold_in(own, position), (shards_of,), jnp.float32, low / len(cuts), top_value / len(cuts)))
        factor_of = factor_of * jnp.repeat(heights, extent[position] // shards_of).reshape([-1 if axis == position else 1 for axis in range(len(extent))])
    return factor_of


def normal_values(key, shape, deviation, bound, split=(), held_as=jnp.bfloat16):
    values = jax.random.normal(key, shape, jnp.float32) * deviation
    if len(split) > 0:
        values = steps_of(key, shape, split, -0.22, 0.18) * values
    return jnp.clip(values, min=-bound, max=bound).astype(held_as)


def setup_inputs(seed: int = 0) -> dict:
    seeds = jax.random.split(jax.random.key(seed), 4)
    pair = normal_values(seeds[0], (N, N, C), 1.0, 6.0, ((0, 16), (1, 16)))
    projection = normal_values(seeds[1], (C, 4 * CH + C), C ** -0.5, 0.5)
    out_weight = normal_values(seeds[2], (CH, C), CH ** -0.5, 0.5)
    return dict(pair=pair, projection=projection, out_weight=out_weight)


epsilon = 1e-05

def layer_norm(values, axis):
    mean_value = lax.optimization_barrier(jnp.mean(values, axis=axis, keepdims=True))
    centered = values - mean_value
    variance = lax.optimization_barrier(jnp.mean(centered * centered, axis=axis, keepdims=True))
    return centered * lax.rsqrt(variance + epsilon)

def project(block, projection):
    normed = layer_norm(block.astype(jnp.float32), -1).astype(jnp.bfloat16)
    projected = jnp.dot(normed.reshape(-1, C), projection, preferred_element_type=jnp.float32)
    projected = projected.reshape(block.shape[0], N, 4 * CH + C)
    left_side = (jax.nn.sigmoid(projected[..., :CH]) * projected[..., CH:2 * CH]).astype(jnp.bfloat16)
    right_side = (jax.nn.sigmoid(projected[..., 2 * CH:3 * CH]) * projected[..., 3 * CH:4 * CH]).astype(jnp.bfloat16)
    gate_value = jax.nn.sigmoid(projected[..., 4 * CH:])
    return (left_side, right_side, gate_value)

def reference(pair, projection, out_weight):
    block_rows = math.gcd(N, 64)
    blocks = pair.reshape(N // block_rows, block_rows, N, C)

    def first(block):
        left_side, right_side, gate_value = project(block, projection)
        return (jnp.transpose(left_side, (2, 0, 1)), jnp.transpose(right_side, (2, 0, 1)))
    left_blocks, right_blocks = lax.map(first, blocks)
    right_all = jnp.transpose(right_blocks, (1, 0, 2, 3)).reshape(CH, N, N).astype(jnp.float32)

    def second(inputs):
        block, left_block = inputs
        gate_value = project(block, projection)[2]
        mixed_block = jnp.einsum('cik,cjk->cij', left_block.astype(jnp.float32), right_all).astype(jnp.bfloat16)
        mixed_rows = jnp.transpose(mixed_block, (1, 2, 0)).astype(jnp.float32)
        normed_mix = layer_norm(mixed_rows, -1).astype(jnp.bfloat16)
        output = jnp.dot(normed_mix.reshape(-1, CH), out_weight, preferred_element_type=jnp.float32)
        output = output.reshape(block_rows, N, C)
        return (gate_value * output).astype(jnp.bfloat16)
    return lax.map(second, (blocks, left_blocks)).reshape(N, N, C)
```

```python
import functools

import jax
import jax.numpy as jnp
from jax import lax
from jax.experimental import pallas as pl
from jax.experimental.pallas import tpu as pltpu
from jax.sharding import PartitionSpec as P

epsilon = 1e-05
MESH = pl.DeviceIdType.MESH
f32, bf16 = jnp.float32, jnp.bfloat16


def dot(a, b, dims):
    return lax.dot_general(a, b, (dims, ((), ())), preferred_element_type=f32)


def halves(first, second):
    return (
        jnp.concatenate([first[:, :64], second[:, :64]], axis=1),
        jnp.concatenate([first[:, 64:], second[:, 64:]], axis=1),
    )


def kernel(
    rows, cols, hidden,
    pair, projection, out_weight, update,
    right_f32, left_f32, normed, gate, weights, right_send, left_send, right_got, left_got,
    right_all, left_all, mixed, mixed_send, mixed_got, mixed_f32,
    send_sem, right_sem, left_sem, twin_sem, mixed_sem,
):
    chips = rows * cols // 2
    half_rows = rows // 2
    row, col = lax.axis_index("row"), lax.axis_index("col")
    core = lax.rem(col, 2)
    half = row // half_rows
    slot_row = lax.rem(row, half_rows)
    mine = row * (cols // 2) + col // 2
    twin = (row, col + 1 - 2 * core)

    barrier = pltpu.get_barrier_semaphore()

    def greet(step, _):
        other_row = lax.rem(row + step // cols, rows)
        other_col = lax.rem(col + lax.rem(step, cols), cols)
        pl.semaphore_signal(barrier, inc=1, device_id=(other_row, other_col), device_id_type=MESH)
        return 0

    lax.fori_loop(1, rows * cols, greet, 0)

    weights[...] = projection[:, : 4 * hidden].T

    def lines(step):
        block, inner = step // 8, lax.rem(step, 8) * 2
        return block * 32 + inner

    def norm_and_right(step, _):
        top = lines(step)
        values = jnp.concatenate(
            [pair[top], pair[top + 16], pair[top + 1], pair[top + 17]], axis=0
        ).astype(f32)
        centered = values - jnp.mean(values, axis=-1, keepdims=True)
        variance = jnp.mean(centered * centered, axis=-1, keepdims=True)
        unit = (centered * lax.rsqrt(variance + epsilon)).astype(bf16)
        normed[step] = unit
        both = dot(weights[2 * hidden : 4 * hidden], unit, ((1,), (1,)))
        side = jax.nn.sigmoid(both[:hidden]) * both[hidden:]
        right_f32[pl.ds(2 * step, hidden, stride=32), :] = side[:, :128]
        right_f32[pl.ds(2 * step + 1, hidden, stride=32), :] = side[:, 128:]
        return 0

    lax.fori_loop(0, 16, norm_and_right, 0)

    pl.semaphore_wait(barrier, rows * cols - 1)

    def target(step):
        other_row = lax.rem(row + step // (cols // 2), rows)
        other_pair = lax.rem(col // 2 + lax.rem(step, cols // 2), cols // 2)
        return other_row, other_pair, other_row * (cols // 2) + other_pair

    def send_side(held, outgoing, got, sem, sent, count, first, size):
        def one(step):
            other_row, other_pair, channel = target(step)
            base = pl.multiple_of(channel * 32 + first, 16)
            outgoing[channel, first : first + size] = held[pl.ds(base, size), :].astype(bf16)
            return outgoing.at[channel, pl.ds(first, size)], (other_row, other_pair * 2 + half)

        source, device = one(0)

        @pl.when(half == core)
        def _():
            pltpu.make_async_copy(source, got, sem).start()

        @pl.when(half != core)
        def _():
            pltpu.make_async_remote_copy(
                src_ref=source, dst_ref=got, send_sem=sent, recv_sem=sem, device_id=twin, device_id_type=MESH
            ).start()

        def body(step, _):
            source, device = one(step)
            pltpu.make_async_remote_copy(
                src_ref=source, dst_ref=got, send_sem=sent, recv_sem=sem, device_id=device, device_id_type=MESH
            ).start()
            return 0

        lax.fori_loop(1, chips, body, 0)

    send_side(right_f32, right_send, right_got.at[half, col, slot_row], right_sem, send_sem.at[0], chips, 0, 32)

    def left_side(step, _):
        both = dot(weights[: 2 * hidden], normed[step], ((1,), (1,)))
        side = jax.nn.sigmoid(both[:hidden]) * both[hidden:]
        left_f32[pl.ds(2 * step, hidden, stride=32), :] = side[:, :128]
        left_f32[pl.ds(2 * step + 1, hidden, stride=32), :] = side[:, 128:]
        return 0

    for part in range(2):
        lax.fori_loop(8 * part, 8 * part + 8, left_side, 0)
        send_side(
            left_f32, left_send, left_got.at[part, col, slot_row], left_sem.at[part], send_sem.at[1 + part],
            chips, 16 * part, 16,
        )

    def gate_of(step, _):
        gate[step] = jax.nn.sigmoid(dot(normed[step], projection[:, 4 * hidden :], ((1,), (0,))))
        return 0

    lax.fori_loop(0, 16, gate_of, 0)

    pltpu.make_async_copy(right_got.at[core], right_got.at[core], right_sem).wait()
    handed = pltpu.make_async_remote_copy(
        src_ref=right_got.at[core], dst_ref=right_got.at[core], send_sem=send_sem.at[3], recv_sem=twin_sem,
        device_id=twin, device_id_type=MESH,
    )
    handed.start()

    def arrange_right(which):
        def body(line, _):
            base = pl.multiple_of((which * half_rows + line) * 64, 64)
            for m in range(cols // 2):
                first, second = right_got[which, 2 * m, line], right_got[which, 2 * m + 1, line]
                low, high = halves(first, second)
                span = slice(128 * m, 128 * m + 128)
                right_all[pl.ds(base, 16), span] = low[:16]
                right_all[pl.ds(base + 16, 16), span] = high[:16]
                right_all[pl.ds(base + 32, 16), span] = low[16:]
                right_all[pl.ds(base + 48, 16), span] = high[16:]
            return 0

        lax.fori_loop(0, half_rows, body, 0)

    arrange_right(core)
    handed.wait_recv()
    arrange_right(1 - core)

    for part in range(2):
        pltpu.make_async_copy(left_got.at[part], left_got.at[part], left_sem.at[part]).wait()

        def arrange_left(line, _):
            base = pl.multiple_of(line * 32, 32)
            for m in range(cols // 2):
                low, high = halves(left_got[part, 2 * m, line], left_got[part, 2 * m + 1, line])
                left_all[pl.ds(base, 16), 128 * m : 128 * m + 128] = low
                left_all[pl.ds(base + 16, 16), 128 * m : 128 * m + 128] = high
            return 0

        lax.fori_loop(0, half_rows, arrange_left, 0)

        def multiply(step, _):
            base = pl.multiple_of(step * 256, 256)
            mixed[...] = dot(left_all[...], right_all[pl.ds(base, 256), :], ((1,), (1,))).astype(bf16)
            for line in range(half_rows):
                for m in range(2):
                    span = slice(128 * m, 128 * m + 128)
                    low, high = halves(mixed[line * 32 : line * 32 + 16, span], mixed[line * 32 + 16 : line * 32 + 32, span])
                    mixed_send[part, line, step * 4 + 2 * m] = low
                    mixed_send[part, line, step * 4 + 2 * m + 1] = high
            return 0

        lax.fori_loop(0, cols // 4, multiply, 0)

        got = mixed_got.at[part, mine]

        def send_mixed(step, _):
            line = lax.rem(slot_row + step // cols, half_rows)
            other = lax.rem(col + lax.rem(step, cols), cols)
            source = mixed_send.at[part, line, other]
            own = jnp.logical_and(step == 0, half == core)

            @pl.when(own)
            def _():
                pltpu.make_async_copy(source, got, mixed_sem.at[part]).start()

            @pl.when(jnp.logical_not(own))
            def _():
                pltpu.make_async_remote_copy(
                    src_ref=source, dst_ref=got, send_sem=send_sem.at[4 + part], recv_sem=mixed_sem.at[part],
                    device_id=(core * half_rows + line, other), device_id_type=MESH,
                ).start()

            return 0

        lax.fori_loop(0, half_rows * cols, send_mixed, 0)

    for part in range(2):
        pltpu.make_async_copy(mixed_got.at[part], mixed_got.at[part], mixed_sem.at[part]).wait()

        total = jnp.zeros((16, 128), f32)
        total = lax.fori_loop(0, hidden, lambda c, t: t + mixed_got[part, c].astype(f32), total)
        mean = total * (1.0 / hidden)

        def square(c, t):
            centered = mixed_got[part, c].astype(f32) - mean
            return t + centered * centered

        scale = lax.rsqrt(lax.fori_loop(0, hidden, square, jnp.zeros((16, 128), f32)) * (1.0 / hidden) + epsilon)

        def norm(c, _):
            mixed_f32[pl.ds(pl.multiple_of(c * 16, 16), 16), :] = (mixed_got[part, c].astype(f32) - mean) * scale
            return 0

        lax.fori_loop(0, hidden, norm, 0)

        def finish(line, _):
            unit = mixed_f32[pl.ds(line, hidden, stride=16), :].astype(bf16)
            product = dot(unit, out_weight[...], ((0,), (0,)))
            step = part * 8 + line // 2
            result = (gate[step, pl.ds(pl.multiple_of(lax.rem(line, 2) * 128, 128), 128), :] * product).astype(bf16)
            update[part * 32 + line] = result[:64]
            update[part * 32 + line + 16] = result[64:]
            return 0

        lax.fori_loop(0, 16, finish, 0)

    sent_bytes = chips - 1 + jnp.where(half == core, 0, 1)

    @pl.when(half == core)
    def _():
        pltpu.make_async_copy(right_send.at[pl.ds(0, chips - 1)], right_send.at[pl.ds(0, chips - 1)], send_sem.at[0]).wait()
        for part in range(2):
            span = left_send.at[pl.ds(0, chips - 1), pl.ds(0, 16)]
            pltpu.make_async_copy(span, span, send_sem.at[1 + part]).wait()
            span = mixed_got.at[0, pl.ds(0, chips - 1)]
            pltpu.make_async_copy(span, span, send_sem.at[4 + part]).wait()

    @pl.when(half != core)
    def _():
        pltpu.make_async_copy(right_send, right_send, send_sem.at[0]).wait()
        for part in range(2):
            span = left_send.at[:, pl.ds(0, 16)]
            pltpu.make_async_copy(span, span, send_sem.at[1 + part]).wait()
            span = mixed_got.at[0]
            pltpu.make_async_copy(span, span, send_sem.at[4 + part]).wait()

    handed.wait_send()


def local(rows, cols, pair, projection, out_weight):
    hidden = out_weight.shape[0]
    half_rows = rows // 2
    vmem = pl.BlockSpec(memory_space=pltpu.VMEM)
    length = cols * 64
    return pl.pallas_call(
        functools.partial(kernel, rows, cols, hidden),
        out_shape=jax.ShapeDtypeStruct(pair.shape, bf16),
        in_specs=[vmem] * 3,
        out_specs=vmem,
        scratch_shapes=[
            pltpu.VMEM((hidden * 32, 128), f32),
            pltpu.VMEM((hidden * 32, 128), f32),
            pltpu.VMEM((16, 256, 128), bf16),
            pltpu.VMEM((16, 256, 128), f32),
            pltpu.VMEM((4 * hidden, 128), bf16),
            pltpu.VMEM((hidden, 32, 128), bf16),
            pltpu.VMEM((hidden, 32, 128), bf16),
            pltpu.VMEM((2, cols, half_rows, 32, 128), bf16),
            pltpu.VMEM((2, cols, half_rows, 16, 128), bf16),
            pltpu.VMEM((rows * 64, length), bf16),
            pltpu.VMEM((half_rows * 32, length), bf16),
            pltpu.VMEM((half_rows * 32, 256), bf16),
            pltpu.VMEM((2, half_rows, cols, 16, 128), bf16),
            pltpu.VMEM((2, hidden, 16, 128), bf16),
            pltpu.VMEM((hidden * 16, 128), f32),
            pltpu.SemaphoreType.DMA((6,)),
            pltpu.SemaphoreType.DMA,
            pltpu.SemaphoreType.DMA((2,)),
            pltpu.SemaphoreType.DMA,
            pltpu.SemaphoreType.DMA((2,)),
        ],
        compiler_params=pltpu.CompilerParams(
            collective_id=0, has_side_effects=True, vmem_limit_bytes=48 * 2**20
        ),
        name="triangle",
    )(pair, projection, out_weight)


def solution(mesh):
    placed = (P("row", "col", None), P(), P())
    rows, cols = mesh.shape["row"], mesh.shape["col"]
    return jax.shard_map(
        functools.partial(local, rows, cols),
        mesh=mesh,
        in_specs=placed,
        out_specs=P("row", "col", None),
        check_vma=False,
    )
```

```python
import functools

import jax
import jax.numpy as jnp
from jax import lax
from jax.experimental import pallas as pl
from jax.experimental.pallas import tpu as pltpu
from jax.sharding import PartitionSpec as P

epsilon = 1e-05
MESH = pl.DeviceIdType.MESH
f32, bf16 = jnp.float32, jnp.bfloat16


def dot(a, b, dims):
    return lax.dot_general(a, b, (dims, ((), ())), preferred_element_type=f32)


def halves(first, second):
    return (
        jnp.concatenate([first[:, :64], second[:, :64]], axis=1),
        jnp.concatenate([first[:, 64:], second[:, 64:]], axis=1),
    )


def kernel(
    rows, cols, hidden,
    pair_hbm, projection_hbm, out_weight_hbm, update,
    pair, projection, out_weight, right_f32, left_f32, normed, gate, weights, right_send, left_send, right_got, left_got,
    right_all, left_all, mixed, mixed_send, mixed_got, mixed_f32,
    load_sem, entered_sem, send_sem, right_sem, left_sem, twin_sem, mixed_sem,
):
    chips = rows * cols // 2
    half_rows = rows // 2
    row, col = lax.axis_index("row"), lax.axis_index("col")
    core = lax.rem(col, 2)
    half = row // half_rows
    slot_row = lax.rem(row, half_rows)
    mine = row * (cols // 2) + col // 2
    twin = (row, col + 1 - 2 * core)

    loads = [
        pltpu.make_async_copy(projection_hbm, projection, load_sem.at[0]),
        pltpu.make_async_copy(pair_hbm.at[pl.ds(0, 32)], pair.at[pl.ds(0, 32)], load_sem.at[1]),
        pltpu.make_async_copy(pair_hbm.at[pl.ds(32, 32)], pair.at[pl.ds(32, 32)], load_sem.at[2]),
        pltpu.make_async_copy(out_weight_hbm, out_weight, load_sem.at[3]),
    ]
    for load in loads:
        load.start()

    barrier = pltpu.get_barrier_semaphore()
    row_peers = [(lax.rem(row + step, rows), col) for step in range(1, rows)]
    col_peers = [(row, lax.rem(col + step, cols)) for step in range(1, cols)]
    for peer in row_peers + col_peers:
        pl.semaphore_signal(barrier, inc=1, device_id=peer, device_id_type=MESH)

    loads[0].wait()
    weights[...] = projection[:, : 4 * hidden].T

    def lines(step):
        block, inner = step // 8, lax.rem(step, 8) * 2
        return block * 32 + inner

    def norm(step, _):
        top = lines(step)
        values = jnp.concatenate(
            [pair[top], pair[top + 16], pair[top + 1], pair[top + 17]], axis=0
        ).astype(f32)
        centered = values - jnp.mean(values, axis=-1, keepdims=True)
        variance = jnp.mean(centered * centered, axis=-1, keepdims=True)
        unit = (centered * lax.rsqrt(variance + epsilon)).astype(bf16)
        normed[step] = unit
        return 0

    def right_side(step, _):
        both = dot(weights[2 * hidden : 4 * hidden], normed[step], ((1,), (1,)))
        side = jax.nn.sigmoid(both[:hidden]) * both[hidden:]
        right_f32[pl.ds(2 * step, hidden, stride=32), :] = side[:, :128]
        right_f32[pl.ds(2 * step + 1, hidden, stride=32), :] = side[:, 128:]
        return 0

    loads[1].wait()
    lax.fori_loop(0, 8, norm, 0, unroll=2)
    pl.semaphore_wait(barrier, rows - 1 + cols - 1)
    for peer in row_peers:
        pl.semaphore_signal(entered_sem, inc=1, device_id=peer, device_id_type=MESH)
    loads[2].wait()
    lax.fori_loop(8, 16, norm, 0, unroll=2)
    lax.fori_loop(0, 16, right_side, 0, unroll=4)
    pl.semaphore_wait(entered_sem, rows - 1)

    def target(step):
        other_row = lax.rem(row + step // (cols // 2), rows)
        other_pair = lax.rem(col // 2 + lax.rem(step, cols // 2), cols // 2)
        return other_row, other_pair, other_row * (cols // 2) + other_pair

    def send_side(held, outgoing, got, sem, sent, first, size):
        def one(step):
            other_row, other_pair, channel = target(step)
            base = pl.multiple_of(channel * 32 + first, 16)
            outgoing[channel, first : first + size] = held[pl.ds(base, size), :].astype(bf16)
            return outgoing.at[channel, pl.ds(first, size)], (other_row, other_pair * 2 + half)

        source, device = one(0)

        @pl.when(half == core)
        def _():
            pltpu.make_async_copy(source, got, sem).start()

        @pl.when(half != core)
        def _():
            pltpu.make_async_remote_copy(
                src_ref=source, dst_ref=got, send_sem=sent, recv_sem=sem, device_id=twin, device_id_type=MESH
            ).start()

        def body(step, _):
            source, device = one(step)
            pltpu.make_async_remote_copy(
                src_ref=source, dst_ref=got, send_sem=sent, recv_sem=sem, device_id=device, device_id_type=MESH
            ).start()
            return 0

        body(1, 0)
        body(2, 0)
        body(3, 0)
        lax.fori_loop(4, chips, body, 0, unroll=4)

    send_side(right_f32, right_send, right_got.at[half, col, slot_row], right_sem, send_sem.at[0], 0, 32)

    def left_side(step, _):
        both = dot(weights[: 2 * hidden], normed[step], ((1,), (1,)))
        side = jax.nn.sigmoid(both[:hidden]) * both[hidden:]
        left_f32[pl.ds(2 * step, hidden, stride=32), :] = side[:, :128]
        left_f32[pl.ds(2 * step + 1, hidden, stride=32), :] = side[:, 128:]
        return 0

    for part in range(2):
        lax.fori_loop(8 * part, 8 * part + 8, left_side, 0, unroll=4)
        send_side(
            left_f32, left_send, left_got.at[part, col, slot_row], left_sem.at[part], send_sem.at[1 + part],
            16 * part, 16,
        )

    def gate_of(step, _):
        gate[step] = jax.nn.sigmoid(dot(normed[step], projection[:, 4 * hidden :], ((1,), (0,))))
        return 0

    lax.fori_loop(0, 16, gate_of, 0, unroll=4)

    pltpu.make_async_copy(right_got.at[core], right_got.at[core], right_sem).wait()
    handed = pltpu.make_async_remote_copy(
        src_ref=right_got.at[core], dst_ref=right_got.at[core], send_sem=send_sem.at[3], recv_sem=twin_sem,
        device_id=twin, device_id_type=MESH,
    )
    handed.start()

    def arrange_right(which):
        def body(line, _):
            base = pl.multiple_of((which * half_rows + line) * 64, 64)
            for m in range(cols // 2):
                first, second = right_got[which, 2 * m, line], right_got[which, 2 * m + 1, line]
                low, high = halves(first, second)
                span = slice(128 * m, 128 * m + 128)
                right_all[pl.ds(base, 16), span] = low[:16]
                right_all[pl.ds(base + 16, 16), span] = high[:16]
                right_all[pl.ds(base + 32, 16), span] = low[16:]
                right_all[pl.ds(base + 48, 16), span] = high[16:]
            return 0

        lax.fori_loop(0, half_rows, body, 0)

    arrange_right(core)
    handed.wait_recv()
    arrange_right(1 - core)

    for part in range(2):
        pltpu.make_async_copy(left_got.at[part], left_got.at[part], left_sem.at[part]).wait()

        def arrange_left(line, _):
            base = pl.multiple_of(line * 32, 32)
            for m in range(cols // 2):
                low, high = halves(left_got[part, 2 * m, line], left_got[part, 2 * m + 1, line])
                left_all[pl.ds(base, 16), 128 * m : 128 * m + 128] = low
                left_all[pl.ds(base + 16, 16), 128 * m : 128 * m + 128] = high
            return 0

        lax.fori_loop(0, half_rows, arrange_left, 0)

        def multiply(step, _):
            base = pl.multiple_of(step * 256, 256)
            mixed[...] = dot(left_all[...], right_all[pl.ds(base, 256), :], ((1,), (1,))).astype(bf16)
            for line in range(half_rows):
                for m in range(2):
                    span = slice(128 * m, 128 * m + 128)
                    low, high = halves(mixed[line * 32 : line * 32 + 16, span], mixed[line * 32 + 16 : line * 32 + 32, span])
                    mixed_send[part, line, step * 4 + 2 * m] = low
                    mixed_send[part, line, step * 4 + 2 * m + 1] = high
            return 0

        lax.fori_loop(0, cols // 4, multiply, 0)

        got = mixed_got.at[part, mine]

        def send_mixed(step, _):
            line = lax.rem(slot_row + step // cols, half_rows)
            other = lax.rem(col + lax.rem(step, cols), cols)
            source = mixed_send.at[part, line, other]
            own = jnp.logical_and(step == 0, half == core)

            @pl.when(own)
            def _():
                pltpu.make_async_copy(source, got, mixed_sem.at[part]).start()

            @pl.when(jnp.logical_not(own))
            def _():
                pltpu.make_async_remote_copy(
                    src_ref=source, dst_ref=got, send_sem=send_sem.at[4 + part], recv_sem=mixed_sem.at[part],
                    device_id=(core * half_rows + line, other), device_id_type=MESH,
                ).start()

            return 0

        lax.fori_loop(0, half_rows * cols, send_mixed, 0, unroll=4)

    loads[3].wait()
    for part in range(2):
        pltpu.make_async_copy(mixed_got.at[part], mixed_got.at[part], mixed_sem.at[part]).wait()

        total = jnp.zeros((16, 128), f32)
        total = lax.fori_loop(0, hidden, lambda c, t: t + mixed_got[part, c].astype(f32), total, unroll=min(16, hidden))
        mean = total * (1.0 / hidden)

        def square(c, t):
            centered = mixed_got[part, c].astype(f32) - mean
            return t + centered * centered

        scale = lax.rsqrt(lax.fori_loop(0, hidden, square, jnp.zeros((16, 128), f32), unroll=min(16, hidden)) * (1.0 / hidden) + epsilon)

        def scaled(c, _):
            mixed_f32[pl.ds(pl.multiple_of(c * 16, 16), 16), :] = (mixed_got[part, c].astype(f32) - mean) * scale
            return 0

        lax.fori_loop(0, hidden, scaled, 0, unroll=min(16, hidden))

        def finish(line, _):
            unit = mixed_f32[pl.ds(line, hidden, stride=16), :].astype(bf16)
            product = dot(unit, out_weight[...], ((0,), (0,)))
            step = part * 8 + line // 2
            result = (gate[step, pl.ds(pl.multiple_of(lax.rem(line, 2) * 128, 128), 128), :] * product).astype(bf16)
            update[part * 32 + line] = result[:64]
            update[part * 32 + line + 16] = result[64:]
            return 0

        lax.fori_loop(0, 16, finish, 0, unroll=8)

    @pl.when(half == core)
    def _():
        pltpu.make_async_copy(right_send.at[pl.ds(0, chips - 1)], right_send.at[pl.ds(0, chips - 1)], send_sem.at[0]).wait()
        for part in range(2):
            span = left_send.at[pl.ds(0, chips - 1), pl.ds(0, 16)]
            pltpu.make_async_copy(span, span, send_sem.at[1 + part]).wait()
            span = mixed_got.at[0, pl.ds(0, chips - 1)]
            pltpu.make_async_copy(span, span, send_sem.at[4 + part]).wait()

    @pl.when(half != core)
    def _():
        pltpu.make_async_copy(right_send, right_send, send_sem.at[0]).wait()
        for part in range(2):
            span = left_send.at[:, pl.ds(0, 16)]
            pltpu.make_async_copy(span, span, send_sem.at[1 + part]).wait()
            span = mixed_got.at[0]
            pltpu.make_async_copy(span, span, send_sem.at[4 + part]).wait()

    handed.wait_send()


def local(rows, cols, pair, projection, out_weight):
    hidden = out_weight.shape[0]
    half_rows = rows // 2
    vmem = pl.BlockSpec(memory_space=pltpu.VMEM)
    length = cols * 64
    return pl.pallas_call(
        functools.partial(kernel, rows, cols, hidden),
        out_shape=jax.ShapeDtypeStruct(pair.shape, bf16),
        in_specs=[pl.BlockSpec(memory_space=pltpu.HBM)] * 3,
        out_specs=vmem,
        scratch_shapes=[
            pltpu.VMEM(pair.shape, bf16),
            pltpu.VMEM(projection.shape, bf16),
            pltpu.VMEM(out_weight.shape, bf16),
            pltpu.VMEM((hidden * 32, 128), f32),
            pltpu.VMEM((hidden * 32, 128), f32),
            pltpu.VMEM((16, 256, 128), bf16),
            pltpu.VMEM((16, 256, 128), f32),
            pltpu.VMEM((4 * hidden, 128), bf16),
            pltpu.VMEM((hidden, 32, 128), bf16),
            pltpu.VMEM((hidden, 32, 128), bf16),
            pltpu.VMEM((2, cols, half_rows, 32, 128), bf16),
            pltpu.VMEM((2, cols, half_rows, 16, 128), bf16),
            pltpu.VMEM((rows * 64, length), bf16),
            pltpu.VMEM((half_rows * 32, length), bf16),
            pltpu.VMEM((half_rows * 32, 256), bf16),
            pltpu.VMEM((2, half_rows, cols, 16, 128), bf16),
            pltpu.VMEM((2, hidden, 16, 128), bf16),
            pltpu.VMEM((hidden * 16, 128), f32),
            pltpu.SemaphoreType.DMA((4,)),
            pltpu.SemaphoreType.REGULAR,
            pltpu.SemaphoreType.DMA((6,)),
            pltpu.SemaphoreType.DMA,
            pltpu.SemaphoreType.DMA((2,)),
            pltpu.SemaphoreType.DMA,
            pltpu.SemaphoreType.DMA((2,)),
        ],
        compiler_params=pltpu.CompilerParams(
            collective_id=0, has_side_effects=True, vmem_limit_bytes=48 * 2**20
        ),
        name="triangle",
    )(pair, projection, out_weight)


def solution(mesh):
    placed = (P("row", "col", None), P(), P())
    rows, cols = mesh.shape["row"], mesh.shape["col"]
    return jax.shard_map(
        functools.partial(local, rows, cols),
        mesh=mesh,
        in_specs=placed,
        out_specs=P("row", "col", None),
        check_vma=False,
    )
```

```python
import functools

import jax
import jax.numpy as jnp
from jax import lax
from jax.experimental import pallas as pl
from jax.experimental.pallas import tpu as pltpu
from jax.sharding import PartitionSpec as P

epsilon = 1e-05
MESH = pl.DeviceIdType.MESH
f32, bf16 = jnp.float32, jnp.bfloat16


def dot(a, b, dims):
    return lax.dot_general(a, b, (dims, ((), ())), preferred_element_type=f32)


def rem(a, b):
    return a % b if isinstance(a, int) else lax.rem(a, b)


def halves(first, second):
    return (
        jnp.concatenate([first[:, :64], second[:, :64]], axis=1),
        jnp.concatenate([first[:, 64:], second[:, 64:]], axis=1),
    )


def kernel(
    rows, cols, hidden,
    pair_hbm, projection_hbm, out_weight_hbm, update_hbm,
    pair, projection, out_weight, update, right_f32, left_f32, normed, gate, weights, right_send, left_send, right_got, left_got,
    right_all, left_all, mixed, mixed_send, mixed_got, mixed_f32,
    load_sem, store_sem, entered_sem, send_sem, right_sem, left_sem, twin_sem, mixed_sem,
):
    chips = rows * cols // 2
    half_rows = rows // 2
    row, col = lax.axis_index("row"), lax.axis_index("col")
    planes, lines_z = rows // 4, 8
    columns = cols // 4
    x, y, z, core = col // 4, row // 4, rem(row, 4) * 2 + rem(col // 2, 2), rem(col, 2)
    half = row // half_rows
    slot_row = rem(row, half_rows)
    mine = row * (cols // 2) + col // 2
    twin = (row, col + 1 - 2 * core)

    def chip(x, y, z):
        return y * 4 + z // 2, x * 2 + rem(z, 2)

    def along_z(k):
        return rem(z + 4 + ((k + 1) // 2) * (1 - 2 * rem(k, 2)) + lines_z, lines_z)

    loads = [
        pltpu.make_async_copy(projection_hbm, projection, load_sem.at[0]),
        pltpu.make_async_copy(pair_hbm.at[pl.ds(0, 32)], pair.at[pl.ds(0, 32)], load_sem.at[1]),
        pltpu.make_async_copy(pair_hbm.at[pl.ds(32, 32)], pair.at[pl.ds(32, 32)], load_sem.at[2]),
        pltpu.make_async_copy(out_weight_hbm, out_weight, load_sem.at[3]),
    ]
    for load in loads:
        load.start()

    barrier = pltpu.get_barrier_semaphore()
    x_peers = [(row, rem(col + 4 * step, cols)) for step in range(1, columns)]
    for k in range(lines_z):
        for step in range(planes):
            place, pair_place = chip(x, rem(y + step, planes), along_z(k))
            if k < lines_z - 1 or step > 0:
                pl.semaphore_signal(barrier, inc=1, device_id=(place, pair_place * 2), device_id_type=MESH)
                pl.semaphore_signal(barrier, inc=1, device_id=(place, pair_place * 2 + 1), device_id_type=MESH)
    for peer in [twin] + x_peers:
        pl.semaphore_signal(barrier, inc=1, device_id=peer, device_id_type=MESH)

    loads[0].wait()
    weights[...] = projection[:, : 4 * hidden].T

    def lines(step):
        block, inner = step // 8, rem(step, 8) * 2
        return block * 32 + inner

    def norm(step, _):
        top = lines(step)
        values = jnp.concatenate(
            [pair[top], pair[top + 16], pair[top + 1], pair[top + 17]], axis=0
        ).astype(f32)
        centered = values - jnp.mean(values, axis=-1, keepdims=True)
        variance = jnp.mean(centered * centered, axis=-1, keepdims=True)
        unit = (centered * lax.rsqrt(variance + epsilon)).astype(bf16)
        normed[step] = unit
        return 0

    def right_side(step, _):
        both = dot(weights[2 * hidden : 4 * hidden], normed[step], ((1,), (1,)))
        side = jax.nn.sigmoid(both[:hidden]) * both[hidden:]
        right_f32[pl.ds(2 * step, hidden, stride=32), :] = side[:, :128]
        right_f32[pl.ds(2 * step + 1, hidden, stride=32), :] = side[:, 128:]
        return 0

    for part in range(2):
        loads[1 + part].wait()
        lax.fori_loop(8 * part, 8 * part + 8, norm, 0, unroll=2)
    lax.fori_loop(0, 16, right_side, 0, unroll=4)

    def send_side(held, outgoing, got, sem, sent, first, size, start, stop):
        def fill(channel):
            base = pl.multiple_of(channel * 32 + first, 16)
            outgoing[channel, first : first + size] = held[pl.ds(base, size), :].astype(bf16)
            return outgoing.at[channel, pl.ds(first, size)]

        def body(step, _):
            place, pair_place = chip(
                rem(x + step // (planes * lines_z), columns),
                rem(y + step // lines_z + 1, planes),
                along_z(rem(step, lines_z)),
            )
            pltpu.make_async_remote_copy(
                src_ref=fill(place * (cols // 2) + pair_place), dst_ref=got, send_sem=sent, recv_sem=sem,
                device_id=(place, pair_place * 2 + half), device_id_type=MESH,
            ).start()
            return 0

        own = planes * lines_z - 1
        if start <= own:
            head = (own - start) % 4
            for step in range(start, start + head):
                body(step, 0)
            lax.fori_loop(start + head, own, body, 0, unroll=4)
            source = fill(mine)

            @pl.when(half == core)
            def _():
                pltpu.make_async_copy(source, got, sem).start()

            @pl.when(half != core)
            def _():
                pltpu.make_async_remote_copy(
                    src_ref=source, dst_ref=got, send_sem=sent, recv_sem=sem, device_id=twin, device_id_type=MESH
                ).start()

            start = own + 1
        lax.fori_loop(start, stop, body, 0, unroll=4)

    right_slot = right_got.at[half, col, slot_row]
    near = planes * lines_z
    pl.semaphore_wait(barrier, 2 * near - 1 + columns - 1)
    for peer in x_peers:
        pl.semaphore_signal(entered_sem, inc=1, device_id=peer, device_id_type=MESH)
    send_side(right_f32, right_send, right_slot, right_sem, send_sem.at[0], 0, 32, 0, near)
    pl.semaphore_wait(entered_sem, columns - 1)
    send_side(right_f32, right_send, right_slot, right_sem, send_sem.at[0], 0, 32, near, chips)

    def left_side(step, _):
        both = dot(weights[: 2 * hidden], normed[step], ((1,), (1,)))
        side = jax.nn.sigmoid(both[:hidden]) * both[hidden:]
        left_f32[pl.ds(2 * step, hidden, stride=32), :] = side[:, :128]
        left_f32[pl.ds(2 * step + 1, hidden, stride=32), :] = side[:, 128:]
        return 0

    for part in range(2):
        lax.fori_loop(8 * part, 8 * part + 8, left_side, 0, unroll=4)
        send_side(
            left_f32, left_send, left_got.at[part, col, slot_row], left_sem.at[part], send_sem.at[1 + part],
            16 * part, 16, 0, chips,
        )

    def gate_of(step, _):
        gate[step] = jax.nn.sigmoid(dot(normed[step], projection[:, 4 * hidden :], ((1,), (0,))))
        return 0

    lax.fori_loop(0, 16, gate_of, 0, unroll=4)

    pltpu.make_async_copy(right_got.at[core], right_got.at[core], right_sem).wait()
    handed = pltpu.make_async_remote_copy(
        src_ref=right_got.at[core], dst_ref=right_got.at[core], send_sem=send_sem.at[3], recv_sem=twin_sem,
        device_id=twin, device_id_type=MESH,
    )
    handed.start()

    def arrange_right(which):
        def body(line, _):
            base = pl.multiple_of((which * half_rows + line) * 64, 64)
            for m in range(cols // 2):
                first, second = right_got[which, 2 * m, line], right_got[which, 2 * m + 1, line]
                low, high = halves(first, second)
                span = slice(128 * m, 128 * m + 128)
                right_all[pl.ds(base, 16), span] = low[:16]
                right_all[pl.ds(base + 16, 16), span] = high[:16]
                right_all[pl.ds(base + 32, 16), span] = low[16:]
                right_all[pl.ds(base + 48, 16), span] = high[16:]
            return 0

        lax.fori_loop(0, half_rows, body, 0)

    arrange_right(core)
    handed.wait_recv()
    arrange_right(1 - core)

    for part in range(2):
        pltpu.make_async_copy(left_got.at[part], left_got.at[part], left_sem.at[part]).wait()

        def arrange_left(line, _):
            base = pl.multiple_of(line * 32, 32)
            for m in range(cols // 2):
                low, high = halves(left_got[part, 2 * m, line], left_got[part, 2 * m + 1, line])
                left_all[pl.ds(base, 16), 128 * m : 128 * m + 128] = low
                left_all[pl.ds(base + 16, 16), 128 * m : 128 * m + 128] = high
            return 0

        lax.fori_loop(0, half_rows, arrange_left, 0)

        def multiply(step, _):
            base = pl.multiple_of(step * 256, 256)
            mixed[...] = dot(left_all[...], right_all[pl.ds(base, 256), :], ((1,), (1,))).astype(bf16)
            for line in range(half_rows):
                for m in range(2):
                    span = slice(128 * m, 128 * m + 128)
                    low, high = halves(mixed[line * 32 : line * 32 + 16, span], mixed[line * 32 + 16 : line * 32 + 32, span])
                    mixed_send[part, line, step * 4 + 2 * m] = low
                    mixed_send[part, line, step * 4 + 2 * m + 1] = high
            return 0

        lax.fori_loop(0, cols // 4, multiply, 0)

        got = mixed_got.at[part, mine]

        def mixed_message(place, other):
            line = rem(place, half_rows)
            return pltpu.make_async_remote_copy(
                src_ref=mixed_send.at[part, line, other], dst_ref=got,
                send_sem=send_sem.at[4 + part], recv_sem=mixed_sem.at[part],
                device_id=(place, other), device_id_type=MESH,
            )

        def send_mixed(step, _):
            k = rem(step, lines_z)
            other_core = rem(core + 1 + step // lines_z, 2)
            other_y = core * (planes // 2) + rem(y + 1 + step // (2 * lines_z), planes // 2)
            other_x = rem(x + 1 + step // (planes * lines_z), columns)
            place, pair_place = chip(other_x, other_y, along_z(k))
            mixed_message(place, pair_place * 2 + other_core).start()
            return 0

        last = chips - 1
        for step in range(3):
            send_mixed(step, 0)
        lax.fori_loop(3, last, send_mixed, 0, unroll=4)
        place = core * half_rows + slot_row

        @pl.when(half == core)
        def _():
            pltpu.make_async_copy(mixed_send.at[part, slot_row, col], got, mixed_sem.at[part]).start()

        @pl.when(half != core)
        def _():
            mixed_message(place, col).start()

    loads[3].wait()
    stores = []
    for part in range(2):
        pltpu.make_async_copy(mixed_got.at[part], mixed_got.at[part], mixed_sem.at[part]).wait()

        total = jnp.zeros((16, 128), f32)
        total = lax.fori_loop(0, hidden, lambda c, t: t + mixed_got[part, c].astype(f32), total, unroll=min(16, hidden))
        mean = total * (1.0 / hidden)

        def square(c, t):
            centered = mixed_got[part, c].astype(f32) - mean
            return t + centered * centered

        scale = lax.rsqrt(lax.fori_loop(0, hidden, square, jnp.zeros((16, 128), f32), unroll=min(16, hidden)) * (1.0 / hidden) + epsilon)

        def scaled(c, _):
            mixed_f32[pl.ds(pl.multiple_of(c * 16, 16), 16), :] = (mixed_got[part, c].astype(f32) - mean) * scale
            return 0

        lax.fori_loop(0, hidden, scaled, 0, unroll=min(16, hidden))

        def finish(line, _):
            unit = mixed_f32[pl.ds(line, hidden, stride=16), :].astype(bf16)
            product = dot(unit, out_weight[...], ((0,), (0,)))
            step = part * 8 + line // 2
            result = (gate[step, pl.ds(pl.multiple_of(rem(line, 2) * 128, 128), 128), :] * product).astype(bf16)
            update[part * 32 + line] = result[:64]
            update[part * 32 + line + 16] = result[64:]
            return 0

        for begin in (0, 8):
            lax.fori_loop(begin, begin + 8, finish, 0, unroll=8)
            for base in (begin, begin + 16):
                span = pl.ds(part * 32 + base, 8)
                stores.append(pltpu.make_async_copy(update.at[span], update_hbm.at[span], store_sem.at[len(stores)]))
                stores[-1].start()

    @pl.when(half == core)
    def _():
        pltpu.make_async_copy(right_send.at[pl.ds(0, chips - 1)], right_send.at[pl.ds(0, chips - 1)], send_sem.at[0]).wait()
        for part in range(2):
            span = left_send.at[pl.ds(0, chips - 1), pl.ds(0, 16)]
            pltpu.make_async_copy(span, span, send_sem.at[1 + part]).wait()
            span = mixed_got.at[0, pl.ds(0, chips - 1)]
            pltpu.make_async_copy(span, span, send_sem.at[4 + part]).wait()

    @pl.when(half != core)
    def _():
        pltpu.make_async_copy(right_send, right_send, send_sem.at[0]).wait()
        for part in range(2):
            span = left_send.at[:, pl.ds(0, 16)]
            pltpu.make_async_copy(span, span, send_sem.at[1 + part]).wait()
            span = mixed_got.at[0]
            pltpu.make_async_copy(span, span, send_sem.at[4 + part]).wait()

    handed.wait_send()
    for store in stores:
        store.wait()


def local(rows, cols, pair, projection, out_weight):
    hidden = out_weight.shape[0]
    half_rows = rows // 2
    length = cols * 64
    return pl.pallas_call(
        functools.partial(kernel, rows, cols, hidden),
        out_shape=jax.ShapeDtypeStruct(pair.shape, bf16),
        in_specs=[pl.BlockSpec(memory_space=pltpu.HBM)] * 3,
        out_specs=pl.BlockSpec(memory_space=pltpu.HBM),
        scratch_shapes=[
            pltpu.VMEM(pair.shape, bf16),
            pltpu.VMEM(projection.shape, bf16),
            pltpu.VMEM(out_weight.shape, bf16),
            pltpu.VMEM(pair.shape, bf16),
            pltpu.VMEM((hidden * 32, 128), f32),
            pltpu.VMEM((hidden * 32, 128), f32),
            pltpu.VMEM((16, 256, 128), bf16),
            pltpu.VMEM((16, 256, 128), f32),
            pltpu.VMEM((4 * hidden, 128), bf16),
            pltpu.VMEM((hidden, 32, 128), bf16),
            pltpu.VMEM((hidden, 32, 128), bf16),
            pltpu.VMEM((2, cols, half_rows, 32, 128), bf16),
            pltpu.VMEM((2, cols, half_rows, 16, 128), bf16),
            pltpu.VMEM((rows * 64, length), bf16),
            pltpu.VMEM((half_rows * 32, length), bf16),
            pltpu.VMEM((half_rows * 32, 256), bf16),
            pltpu.VMEM((2, half_rows, cols, 16, 128), bf16),
            pltpu.VMEM((2, hidden, 16, 128), bf16),
            pltpu.VMEM((hidden * 16, 128), f32),
            pltpu.SemaphoreType.DMA((4,)),
            pltpu.SemaphoreType.DMA((8,)),
            pltpu.SemaphoreType.REGULAR,
            pltpu.SemaphoreType.DMA((6,)),
            pltpu.SemaphoreType.DMA,
            pltpu.SemaphoreType.DMA((2,)),
            pltpu.SemaphoreType.DMA,
            pltpu.SemaphoreType.DMA((2,)),
        ],
        compiler_params=pltpu.CompilerParams(
            collective_id=0, has_side_effects=True, vmem_limit_bytes=58 * 2**20
        ),
        name="triangle",
    )(pair, projection, out_weight)


def solution(mesh):
    placed = (P("row", "col", None), P(), P())
    rows, cols = mesh.shape["row"], mesh.shape["col"]
    return jax.shard_map(
        functools.partial(local, rows, cols),
        mesh=mesh,
        in_specs=placed,
        out_specs=P("row", "col", None),
        check_vma=False,
    )
```

```python
import functools

import jax
import jax.numpy as jnp
from jax import lax
from jax.experimental import pallas as pl
from jax.experimental.pallas import tpu as pltpu
from jax.sharding import PartitionSpec as P

epsilon = 1e-05
MESH = pl.DeviceIdType.MESH
f32, bf16 = jnp.float32, jnp.bfloat16


def dot(a, b, dims):
    return lax.dot_general(a, b, (dims, ((), ())), preferred_element_type=f32)


def rem(a, b):
    return a % b if isinstance(a, int) else lax.rem(a, b)


def halves(first, second):
    return (
        jnp.concatenate([first[:, :64], second[:, :64]], axis=1),
        jnp.concatenate([first[:, 64:], second[:, 64:]], axis=1),
    )


def kernel(
    rows, cols, hidden,
    pair_hbm, projection_hbm, out_weight_hbm, update,
    pair, projection, out_weight, right_f32, left_f32, normed, gate, weights, right_send, left_send, right_got, left_got,
    right_all, left_all, mixed, mixed_send, mixed_got, mixed_f32,
    load_sem, entered_sem, send_sem, right_sem, left_sem, twin_sem, mixed_sem,
):
    chips = rows * cols // 2
    half_rows = rows // 2
    row, col = lax.axis_index("row"), lax.axis_index("col")
    planes, lines_z = rows // 4, 8
    columns = cols // 4
    x, y, z, core = col // 4, row // 4, rem(row, 4) * 2 + rem(col // 2, 2), rem(col, 2)
    half = row // half_rows
    slot_row = rem(row, half_rows)
    mine = row * (cols // 2) + col // 2
    twin = (row, col + 1 - 2 * core)

    def chip(x, y, z):
        return y * 4 + z // 2, x * 2 + rem(z, 2)

    def along_z(k):
        return rem(z + 4 + ((k + 1) // 2) * (1 - 2 * rem(k, 2)) + lines_z, lines_z)

    loads = [
        pltpu.make_async_copy(projection_hbm, projection, load_sem.at[0]),
        pltpu.make_async_copy(pair_hbm.at[pl.ds(0, 32)], pair.at[pl.ds(0, 32)], load_sem.at[1]),
        pltpu.make_async_copy(pair_hbm.at[pl.ds(32, 32)], pair.at[pl.ds(32, 32)], load_sem.at[2]),
        pltpu.make_async_copy(out_weight_hbm, out_weight, load_sem.at[3]),
    ]
    for load in loads:
        load.start()

    barrier = pltpu.get_barrier_semaphore()
    x_peers = [(row, rem(col + 4 * step, cols)) for step in range(1, columns)]
    for k in range(lines_z):
        for step in range(planes):
            place, pair_place = chip(x, rem(y + step, planes), along_z(k))
            if k < lines_z - 1 or step > 0:
                pl.semaphore_signal(barrier, inc=1, device_id=(place, pair_place * 2), device_id_type=MESH)
                pl.semaphore_signal(barrier, inc=1, device_id=(place, pair_place * 2 + 1), device_id_type=MESH)
    for peer in [twin] + x_peers:
        pl.semaphore_signal(barrier, inc=1, device_id=peer, device_id_type=MESH)

    loads[0].wait()
    weights[...] = projection[:, : 4 * hidden].T

    def lines(step):
        block, inner = step // 8, rem(step, 8) * 2
        return block * 32 + inner

    def norm(step, _):
        top = lines(step)
        values = jnp.concatenate(
            [pair[top], pair[top + 16], pair[top + 1], pair[top + 17]], axis=0
        ).astype(f32)
        centered = values - jnp.mean(values, axis=-1, keepdims=True)
        variance = jnp.mean(centered * centered, axis=-1, keepdims=True)
        unit = (centered * lax.rsqrt(variance + epsilon)).astype(bf16)
        normed[step] = unit
        return 0

    def right_side(step, _):
        both = dot(weights[2 * hidden : 4 * hidden], normed[step], ((1,), (1,)))
        side = jax.nn.sigmoid(both[:hidden]) * both[hidden:]
        right_f32[pl.ds(2 * step, hidden, stride=32), :] = side[:, :128]
        right_f32[pl.ds(2 * step + 1, hidden, stride=32), :] = side[:, 128:]
        return 0

    for part in range(2):
        loads[1 + part].wait()
        lax.fori_loop(8 * part, 8 * part + 8, norm, 0, unroll=2)
    lax.fori_loop(0, 16, right_side, 0, unroll=4)

    def send_side(held, outgoing, got, sem, sent, first, size, start, stop):
        def fill(channel):
            base = pl.multiple_of(channel * 32 + first, 16)
            outgoing[channel, first : first + size] = held[pl.ds(base, size), :].astype(bf16)
            return outgoing.at[channel, pl.ds(first, size)]

        def body(step, _):
            place, pair_place = chip(
                rem(x + step // (planes * lines_z), columns),
                rem(y + step // lines_z + 1, planes),
                along_z(rem(step, lines_z)),
            )
            pltpu.make_async_remote_copy(
                src_ref=fill(place * (cols // 2) + pair_place), dst_ref=got, send_sem=sent, recv_sem=sem,
                device_id=(place, pair_place * 2 + half), device_id_type=MESH,
            ).start()
            return 0

        own = planes * lines_z - 1
        if start <= own:
            head = (own - start) % 4
            for step in range(start, start + head):
                body(step, 0)
            lax.fori_loop(start + head, own, body, 0, unroll=4)
            source = fill(mine)

            @pl.when(half == core)
            def _():
                pltpu.make_async_copy(source, got, sem).start()

            @pl.when(half != core)
            def _():
                pltpu.make_async_remote_copy(
                    src_ref=source, dst_ref=got, send_sem=sent, recv_sem=sem, device_id=twin, device_id_type=MESH
                ).start()

            start = own + 1
        lax.fori_loop(start, stop, body, 0, unroll=4)

    right_slot = right_got.at[half, col, slot_row]
    near = planes * lines_z
    pl.semaphore_wait(barrier, 2 * near - 1 + columns - 1)
    for peer in x_peers:
        pl.semaphore_signal(entered_sem, inc=1, device_id=peer, device_id_type=MESH)
    send_side(right_f32, right_send, right_slot, right_sem, send_sem.at[0], 0, 32, 0, near)
    pl.semaphore_wait(entered_sem, columns - 1)
    send_side(right_f32, right_send, right_slot, right_sem, send_sem.at[0], 0, 32, near, chips)

    def left_side(step, _):
        both = dot(weights[: 2 * hidden], normed[step], ((1,), (1,)))
        side = jax.nn.sigmoid(both[:hidden]) * both[hidden:]
        left_f32[pl.ds(2 * step, hidden, stride=32), :] = side[:, :128]
        left_f32[pl.ds(2 * step + 1, hidden, stride=32), :] = side[:, 128:]
        return 0

    for part in range(2):
        lax.fori_loop(8 * part, 8 * part + 8, left_side, 0, unroll=4)
        send_side(
            left_f32, left_send, left_got.at[part, col, slot_row], left_sem.at[part], send_sem.at[1 + part],
            16 * part, 16, 0, chips,
        )

    def gate_of(step, _):
        gate[step] = jax.nn.sigmoid(dot(normed[step], projection[:, 4 * hidden :], ((1,), (0,))))
        return 0

    lax.fori_loop(0, 16, gate_of, 0, unroll=4)

    pltpu.make_async_copy(right_got.at[core], right_got.at[core], right_sem).wait()
    handed = pltpu.make_async_remote_copy(
        src_ref=right_got.at[core], dst_ref=right_got.at[core], send_sem=send_sem.at[3], recv_sem=twin_sem,
        device_id=twin, device_id_type=MESH,
    )
    handed.start()

    def arrange_right(which):
        def body(line, _):
            base = pl.multiple_of((which * half_rows + line) * 64, 64)
            for m in range(cols // 2):
                first, second = right_got[which, 2 * m, line], right_got[which, 2 * m + 1, line]
                low, high = halves(first, second)
                span = slice(128 * m, 128 * m + 128)
                right_all[pl.ds(base, 16), span] = low[:16]
                right_all[pl.ds(base + 16, 16), span] = high[:16]
                right_all[pl.ds(base + 32, 16), span] = low[16:]
                right_all[pl.ds(base + 48, 16), span] = high[16:]
            return 0

        lax.fori_loop(0, half_rows, body, 0)

    arrange_right(core)
    handed.wait_recv()
    arrange_right(1 - core)

    for part in range(2):
        pltpu.make_async_copy(left_got.at[part], left_got.at[part], left_sem.at[part]).wait()

        def arrange_left(line, _):
            base = pl.multiple_of(line * 32, 32)
            for m in range(cols // 2):
                low, high = halves(left_got[part, 2 * m, line], left_got[part, 2 * m + 1, line])
                left_all[pl.ds(base, 16), 128 * m : 128 * m + 128] = low
                left_all[pl.ds(base + 16, 16), 128 * m : 128 * m + 128] = high
            return 0

        lax.fori_loop(0, half_rows, arrange_left, 0)

        def multiply(step, _):
            base = pl.multiple_of(step * 256, 256)
            mixed[...] = dot(left_all[...], right_all[pl.ds(base, 256), :], ((1,), (1,))).astype(bf16)
            for line in range(half_rows):
                for m in range(2):
                    span = slice(128 * m, 128 * m + 128)
                    low, high = halves(mixed[line * 32 : line * 32 + 16, span], mixed[line * 32 + 16 : line * 32 + 32, span])
                    mixed_send[part, line, step * 4 + 2 * m] = low
                    mixed_send[part, line, step * 4 + 2 * m + 1] = high
            return 0

        lax.fori_loop(0, cols // 4, multiply, 0)

        got = mixed_got.at[part, mine]

        def mixed_message(place, other):
            line = rem(place, half_rows)
            return pltpu.make_async_remote_copy(
                src_ref=mixed_send.at[part, line, other], dst_ref=got,
                send_sem=send_sem.at[4 + part], recv_sem=mixed_sem.at[part],
                device_id=(place, other), device_id_type=MESH,
            )

        def send_mixed(step, _):
            k = rem(step, lines_z)
            other_core = rem(core + 1 + step // lines_z, 2)
            other_y = core * (planes // 2) + rem(y + 1 + step // (2 * lines_z), planes // 2)
            other_x = rem(x + 1 + step // (planes * lines_z), columns)
            place, pair_place = chip(other_x, other_y, along_z(k))
            mixed_message(place, pair_place * 2 + other_core).start()
            return 0

        last = chips - 1
        for step in range(3):
            send_mixed(step, 0)
        lax.fori_loop(3, last, send_mixed, 0, unroll=4)
        place = core * half_rows + slot_row

        @pl.when(half == core)
        def _():
            pltpu.make_async_copy(mixed_send.at[part, slot_row, col], got, mixed_sem.at[part]).start()

        @pl.when(half != core)
        def _():
            mixed_message(place, col).start()

    loads[3].wait()
    for part in range(2):
        pltpu.make_async_copy(mixed_got.at[part], mixed_got.at[part], mixed_sem.at[part]).wait()

        total = jnp.zeros((16, 128), f32)
        total = lax.fori_loop(0, hidden, lambda c, t: t + mixed_got[part, c].astype(f32), total, unroll=min(16, hidden))
        mean = total * (1.0 / hidden)

        def square(c, t):
            centered = mixed_got[part, c].astype(f32) - mean
            return t + centered * centered

        scale = lax.rsqrt(lax.fori_loop(0, hidden, square, jnp.zeros((16, 128), f32), unroll=min(16, hidden)) * (1.0 / hidden) + epsilon)

        def scaled(c, _):
            mixed_f32[pl.ds(pl.multiple_of(c * 16, 16), 16), :] = (mixed_got[part, c].astype(f32) - mean) * scale
            return 0

        lax.fori_loop(0, hidden, scaled, 0, unroll=min(16, hidden))

        def finish(line, _):
            unit = mixed_f32[pl.ds(line, hidden, stride=16), :].astype(bf16)
            product = dot(unit, out_weight[...], ((0,), (0,)))
            step = part * 8 + line // 2
            result = (gate[step, pl.ds(pl.multiple_of(rem(line, 2) * 128, 128), 128), :] * product).astype(bf16)
            update[part * 32 + line] = result[:64]
            update[part * 32 + line + 16] = result[64:]
            return 0

        lax.fori_loop(0, 16, finish, 0, unroll=8)

    @pl.when(half == core)
    def _():
        pltpu.make_async_copy(right_send.at[pl.ds(0, chips - 1)], right_send.at[pl.ds(0, chips - 1)], send_sem.at[0]).wait()
        for part in range(2):
            span = left_send.at[pl.ds(0, chips - 1), pl.ds(0, 16)]
            pltpu.make_async_copy(span, span, send_sem.at[1 + part]).wait()
            span = mixed_got.at[0, pl.ds(0, chips - 1)]
            pltpu.make_async_copy(span, span, send_sem.at[4 + part]).wait()

    @pl.when(half != core)
    def _():
        pltpu.make_async_copy(right_send, right_send, send_sem.at[0]).wait()
        for part in range(2):
            span = left_send.at[:, pl.ds(0, 16)]
            pltpu.make_async_copy(span, span, send_sem.at[1 + part]).wait()
            span = mixed_got.at[0]
            pltpu.make_async_copy(span, span, send_sem.at[4 + part]).wait()

    handed.wait_send()


def local(rows, cols, pair, projection, out_weight):
    hidden = out_weight.shape[0]
    half_rows = rows // 2
    vmem = pl.BlockSpec(memory_space=pltpu.VMEM)
    length = cols * 64
    return pl.pallas_call(
        functools.partial(kernel, rows, cols, hidden),
        out_shape=jax.ShapeDtypeStruct(pair.shape, bf16),
        in_specs=[pl.BlockSpec(memory_space=pltpu.HBM)] * 3,
        out_specs=vmem,
        scratch_shapes=[
            pltpu.VMEM(pair.shape, bf16),
            pltpu.VMEM(projection.shape, bf16),
            pltpu.VMEM(out_weight.shape, bf16),
            pltpu.VMEM((hidden * 32, 128), f32),
            pltpu.VMEM((hidden * 32, 128), f32),
            pltpu.VMEM((16, 256, 128), bf16),
            pltpu.VMEM((16, 256, 128), f32),
            pltpu.VMEM((4 * hidden, 128), bf16),
            pltpu.VMEM((hidden, 32, 128), bf16),
            pltpu.VMEM((hidden, 32, 128), bf16),
            pltpu.VMEM((2, cols, half_rows, 32, 128), bf16),
            pltpu.VMEM((2, cols, half_rows, 16, 128), bf16),
            pltpu.VMEM((rows * 64, length), bf16),
            pltpu.VMEM((half_rows * 32, length), bf16),
            pltpu.VMEM((half_rows * 32, 256), bf16),
            pltpu.VMEM((2, half_rows, cols, 16, 128), bf16),
            pltpu.VMEM((2, hidden, 16, 128), bf16),
            pltpu.VMEM((hidden * 16, 128), f32),
            pltpu.SemaphoreType.DMA((4,)),
            pltpu.SemaphoreType.REGULAR,
            pltpu.SemaphoreType.DMA((6,)),
            pltpu.SemaphoreType.DMA,
            pltpu.SemaphoreType.DMA((2,)),
            pltpu.SemaphoreType.DMA,
            pltpu.SemaphoreType.DMA((2,)),
        ],
        compiler_params=pltpu.CompilerParams(
            collective_id=0, has_side_effects=True, vmem_limit_bytes=48 * 2**20
        ),
        name="triangle",
    )(*[pltpu.with_memory_space_constraint(x, pltpu.HBM) for x in (pair, projection, out_weight)])


def solution(mesh):
    placed = (P("row", "col", None), P(), P())
    rows, cols = mesh.shape["row"], mesh.shape["col"]
    return jax.shard_map(
        functools.partial(local, rows, cols),
        mesh=mesh,
        in_specs=placed,
        out_specs=P("row", "col", None),
        check_vma=False,
    )
```

```python
import functools

import jax
import jax.numpy as jnp
from jax import lax
from jax.experimental import pallas as pl
from jax.experimental.pallas import tpu as pltpu
from jax.sharding import PartitionSpec as P

epsilon = 1e-05
MESH = pl.DeviceIdType.MESH
f32, bf16 = jnp.float32, jnp.bfloat16


def dot(a, b, dims):
    return lax.dot_general(a, b, (dims, ((), ())), preferred_element_type=f32)


def rem(a, b):
    return a % b if isinstance(a, int) else lax.rem(a, b)


def halves(first, second):
    return (
        jnp.concatenate([first[:, :64], second[:, :64]], axis=1),
        jnp.concatenate([first[:, 64:], second[:, 64:]], axis=1),
    )


def kernel(
    rows, cols, hidden,
    pair_hbm, projection_hbm, out_weight_hbm, update,
    pair, projection, out_weight, right_f32, left_f32, normed, gate, weights, right_send, left_send, right_got, left_got,
    right_all, left_all, mixed, mixed_send, mixed_got, mixed_f32,
    load_sem, entered_sem, send_sem, right_sem, left_sem, twin_sem, mixed_sem,
):
    chips = rows * cols // 2
    half_rows = rows // 2
    row, col = lax.axis_index("row"), lax.axis_index("col")
    planes, lines_z = rows // 4, 8
    columns = cols // 4
    x, y, z, core = col // 4, row // 4, rem(row, 4) * 2 + rem(col // 2, 2), rem(col, 2)
    half = row // half_rows
    slot_row = rem(row, half_rows)
    mine = row * (cols // 2) + col // 2
    twin = (row, col + 1 - 2 * core)

    def chip(x, y, z):
        return y * 4 + z // 2, x * 2 + rem(z, 2)

    def other(place, k, count):
        return rem(place + count // 2 + ((k + 1) // 2) * (1 - 2 * rem(k, 2)) + count, count)

    loads = [
        pltpu.make_async_copy(projection_hbm, projection, load_sem.at[0]),
        pltpu.make_async_copy(pair_hbm.at[pl.ds(0, 32)], pair.at[pl.ds(0, 32)], load_sem.at[1]),
        pltpu.make_async_copy(pair_hbm.at[pl.ds(32, 32)], pair.at[pl.ds(32, 32)], load_sem.at[2]),
        pltpu.make_async_copy(out_weight_hbm, out_weight, load_sem.at[3]),
    ]
    for load in loads:
        load.start()

    near = planes * lines_z
    barrier = pltpu.get_barrier_semaphore()
    x_peers = [(row, rem(col + 4 * step, cols)) for step in range(1, columns)]
    for k in range(lines_z):
        for step in range(planes):
            place, pair_place = chip(x, other(y, step, planes), other(z, k, lines_z))
            if k < lines_z - 1 or step < planes - 1:
                pl.semaphore_signal(barrier, inc=1, device_id=(place, pair_place * 2), device_id_type=MESH)
                pl.semaphore_signal(barrier, inc=1, device_id=(place, pair_place * 2 + 1), device_id_type=MESH)
    for peer in [twin] + x_peers:
        pl.semaphore_signal(barrier, inc=1, device_id=peer, device_id_type=MESH)

    loads[0].wait()
    weights[...] = projection[:, : 4 * hidden].T

    def lines(step):
        block, inner = step // 8, rem(step, 8) * 2
        return block * 32 + inner

    def norm(step, _):
        top = lines(step)
        values = jnp.concatenate(
            [pair[top], pair[top + 16], pair[top + 1], pair[top + 17]], axis=0
        ).astype(f32)
        centered = values - jnp.mean(values, axis=-1, keepdims=True)
        variance = jnp.mean(centered * centered, axis=-1, keepdims=True)
        unit = (centered * lax.rsqrt(variance + epsilon)).astype(bf16)
        normed[step] = unit
        return 0

    def right_side(step, _):
        both = dot(weights[2 * hidden : 4 * hidden], normed[step], ((1,), (1,)))
        side = jax.nn.sigmoid(both[:hidden]) * both[hidden:]
        right_f32[pl.ds(2 * step, hidden, stride=32), :] = side[:, :128]
        right_f32[pl.ds(2 * step + 1, hidden, stride=32), :] = side[:, 128:]
        return 0

    def send_side(held, outgoing, got, sem, sent, first, stop, apart_too, with_own):
        def fill(channel):
            base = pl.multiple_of(channel * 32 + first, 16)
            outgoing[channel, first : first + 16] = held[pl.ds(base, 16), :].astype(bf16)
            return outgoing.at[channel, pl.ds(first, 16)]

        def body(step, _):
            apart = step // near
            place, pair_place = chip(
                other(x, apart, columns) if apart_too else x,
                other(y, rem(step // lines_z, planes), planes),
                other(z, rem(step, lines_z), lines_z),
            )
            pltpu.make_async_remote_copy(
                src_ref=fill(place * (cols // 2) + pair_place), dst_ref=got, send_sem=sent, recv_sem=sem,
                device_id=(place, pair_place * 2 + half), device_id_type=MESH,
            ).start()
            return 0

        own = stop - 1 if with_own else stop
        for step in range(0, own % 4):
            body(step, 0)
        lax.fori_loop(own % 4, own, body, 0, unroll=4)
        if with_own:
            source = fill(mine)

            @pl.when(half == core)
            def _():
                pltpu.make_async_copy(source, got, sem).start()

            @pl.when(half != core)
            def _():
                pltpu.make_async_remote_copy(
                    src_ref=source, dst_ref=got, send_sem=sent, recv_sem=sem, device_id=twin, device_id_type=MESH
                ).start()

    def send_right(part, stop, apart_too, with_own):
        got = right_got.at[half, col, slot_row, pl.ds(16 * part, 16)]
        send_side(right_f32, right_send, got, right_sem, send_sem.at[0], 16 * part, stop, apart_too, with_own)

    for part in range(2):
        loads[1 + part].wait()
        lax.fori_loop(8 * part, 8 * part + 8, norm, 0, unroll=2)
        lax.fori_loop(8 * part, 8 * part + 8, right_side, 0, unroll=4)
        if part == 0:
            pl.semaphore_wait(barrier, 2 * near - 1 + columns - 1)
            for peer in x_peers:
                pl.semaphore_signal(entered_sem, inc=1, device_id=peer, device_id_type=MESH)
        send_right(part, near, False, True)
    pl.semaphore_wait(entered_sem, columns - 1)
    for part in range(2):
        send_right(part, chips - near, True, False)

    def left_side(step, _):
        both = dot(weights[: 2 * hidden], normed[step], ((1,), (1,)))
        side = jax.nn.sigmoid(both[:hidden]) * both[hidden:]
        left_f32[pl.ds(2 * step, hidden, stride=32), :] = side[:, :128]
        left_f32[pl.ds(2 * step + 1, hidden, stride=32), :] = side[:, 128:]
        return 0

    for part in range(2):
        lax.fori_loop(8 * part, 8 * part + 8, left_side, 0, unroll=4)
        send_side(
            left_f32, left_send, left_got.at[part, col, slot_row], left_sem.at[part], send_sem.at[1 + part],
            16 * part, chips, True, True,
        )

    def gate_of(step, _):
        gate[step] = jax.nn.sigmoid(dot(normed[step], projection[:, 4 * hidden :], ((1,), (0,))))
        return 0

    lax.fori_loop(0, 16, gate_of, 0, unroll=4)

    pltpu.make_async_copy(right_got.at[core], right_got.at[core], right_sem).wait()
    handed = pltpu.make_async_remote_copy(
        src_ref=right_got.at[core], dst_ref=right_got.at[core], send_sem=send_sem.at[3], recv_sem=twin_sem,
        device_id=twin, device_id_type=MESH,
    )
    handed.start()

    def arrange_right(which):
        def body(line, _):
            base = pl.multiple_of((which * half_rows + line) * 64, 64)
            for m in range(cols // 2):
                first, second = right_got[which, 2 * m, line], right_got[which, 2 * m + 1, line]
                low, high = halves(first, second)
                span = slice(128 * m, 128 * m + 128)
                right_all[pl.ds(base, 16), span] = low[:16]
                right_all[pl.ds(base + 16, 16), span] = high[:16]
                right_all[pl.ds(base + 32, 16), span] = low[16:]
                right_all[pl.ds(base + 48, 16), span] = high[16:]
            return 0

        lax.fori_loop(0, half_rows, body, 0)

    arrange_right(core)
    handed.wait_recv()
    arrange_right(1 - core)

    for part in range(2):
        pltpu.make_async_copy(left_got.at[part], left_got.at[part], left_sem.at[part]).wait()

        def arrange_left(line, _):
            base = pl.multiple_of(line * 32, 32)
            for m in range(cols // 2):
                low, high = halves(left_got[part, 2 * m, line], left_got[part, 2 * m + 1, line])
                left_all[pl.ds(base, 16), 128 * m : 128 * m + 128] = low
                left_all[pl.ds(base + 16, 16), 128 * m : 128 * m + 128] = high
            return 0

        lax.fori_loop(0, half_rows, arrange_left, 0)

        def multiply(step, _):
            base = pl.multiple_of(step * 256, 256)
            mixed[...] = dot(left_all[...], right_all[pl.ds(base, 256), :], ((1,), (1,))).astype(bf16)
            for line in range(half_rows):
                for m in range(2):
                    span = slice(128 * m, 128 * m + 128)
                    low, high = halves(mixed[line * 32 : line * 32 + 16, span], mixed[line * 32 + 16 : line * 32 + 32, span])
                    mixed_send[part, line, step * 4 + 2 * m] = low
                    mixed_send[part, line, step * 4 + 2 * m + 1] = high
            return 0

        lax.fori_loop(0, cols // 4, multiply, 0)

        got = mixed_got.at[part, mine]

        def mixed_message(place, to):
            line = rem(place, half_rows)
            return pltpu.make_async_remote_copy(
                src_ref=mixed_send.at[part, line, to], dst_ref=got,
                send_sem=send_sem.at[4 + part], recv_sem=mixed_sem.at[part],
                device_id=(place, to), device_id_type=MESH,
            )

        def send_mixed(step, _):
            other_core = other(core, rem(step // lines_z, 2), 2)
            other_y = core * (planes // 2) + other(rem(y, planes // 2), rem(step // (2 * lines_z), planes // 2), planes // 2)
            other_x = other(x, step // near, columns)
            place, pair_place = chip(other_x, other_y, other(z, rem(step, lines_z), lines_z))
            mixed_message(place, pair_place * 2 + other_core).start()
            return 0

        last = chips - 1
        for step in range(3):
            send_mixed(step, 0)
        lax.fori_loop(3, last, send_mixed, 0, unroll=4)
        place = core * half_rows + slot_row

        @pl.when(half == core)
        def _():
            pltpu.make_async_copy(mixed_send.at[part, slot_row, col], got, mixed_sem.at[part]).start()

        @pl.when(half != core)
        def _():
            mixed_message(place, col).start()

    loads[3].wait()
    for part in range(2):
        pltpu.make_async_copy(mixed_got.at[part], mixed_got.at[part], mixed_sem.at[part]).wait()

        total = jnp.zeros((16, 128), f32)
        total = lax.fori_loop(0, hidden, lambda c, t: t + mixed_got[part, c].astype(f32), total, unroll=min(16, hidden))
        mean = total * (1.0 / hidden)

        def square(c, t):
            centered = mixed_got[part, c].astype(f32) - mean
            return t + centered * centered

        scale = lax.rsqrt(lax.fori_loop(0, hidden, square, jnp.zeros((16, 128), f32), unroll=min(16, hidden)) * (1.0 / hidden) + epsilon)

        def scaled(c, _):
            mixed_f32[pl.ds(pl.multiple_of(c * 16, 16), 16), :] = (mixed_got[part, c].astype(f32) - mean) * scale
            return 0

        lax.fori_loop(0, hidden, scaled, 0, unroll=min(16, hidden))

        def finish(line, _):
            unit = mixed_f32[pl.ds(line, hidden, stride=16), :].astype(bf16)
            product = dot(unit, out_weight[...], ((0,), (0,)))
            step = part * 8 + line // 2
            result = (gate[step, pl.ds(pl.multiple_of(rem(line, 2) * 128, 128), 128), :] * product).astype(bf16)
            update[part * 32 + line] = result[:64]
            update[part * 32 + line + 16] = result[64:]
            return 0

        lax.fori_loop(0, 16, finish, 0, unroll=8)

    @pl.when(half == core)
    def _():
        pltpu.make_async_copy(right_send.at[pl.ds(0, chips - 1)], right_send.at[pl.ds(0, chips - 1)], send_sem.at[0]).wait()
        for part in range(2):
            span = left_send.at[pl.ds(0, chips - 1), pl.ds(0, 16)]
            pltpu.make_async_copy(span, span, send_sem.at[1 + part]).wait()
            span = mixed_got.at[0, pl.ds(0, chips - 1)]
            pltpu.make_async_copy(span, span, send_sem.at[4 + part]).wait()

    @pl.when(half != core)
    def _():
        pltpu.make_async_copy(right_send, right_send, send_sem.at[0]).wait()
        for part in range(2):
            span = left_send.at[:, pl.ds(0, 16)]
            pltpu.make_async_copy(span, span, send_sem.at[1 + part]).wait()
            span = mixed_got.at[0]
            pltpu.make_async_copy(span, span, send_sem.at[4 + part]).wait()

    handed.wait_send()


def local(rows, cols, pair, projection, out_weight):
    hidden = out_weight.shape[0]
    half_rows = rows // 2
    vmem = pl.BlockSpec(memory_space=pltpu.VMEM)
    length = cols * 64
    return pl.pallas_call(
        functools.partial(kernel, rows, cols, hidden),
        out_shape=jax.ShapeDtypeStruct(pair.shape, bf16),
        in_specs=[pl.BlockSpec(memory_space=pltpu.HBM)] * 3,
        out_specs=vmem,
        scratch_shapes=[
            pltpu.VMEM(pair.shape, bf16),
            pltpu.VMEM(projection.shape, bf16),
            pltpu.VMEM(out_weight.shape, bf16),
            pltpu.VMEM((hidden * 32, 128), f32),
            pltpu.VMEM((hidden * 32, 128), f32),
            pltpu.VMEM((16, 256, 128), bf16),
            pltpu.VMEM((16, 256, 128), f32),
            pltpu.VMEM((4 * hidden, 128), bf16),
            pltpu.VMEM((hidden, 32, 128), bf16),
            pltpu.VMEM((hidden, 32, 128), bf16),
            pltpu.VMEM((2, cols, half_rows, 32, 128), bf16),
            pltpu.VMEM((2, cols, half_rows, 16, 128), bf16),
            pltpu.VMEM((rows * 64, length), bf16),
            pltpu.VMEM((half_rows * 32, length), bf16),
            pltpu.VMEM((half_rows * 32, 256), bf16),
            pltpu.VMEM((2, half_rows, cols, 16, 128), bf16),
            pltpu.VMEM((2, hidden, 16, 128), bf16),
            pltpu.VMEM((hidden * 16, 128), f32),
            pltpu.SemaphoreType.DMA((4,)),
            pltpu.SemaphoreType.REGULAR,
            pltpu.SemaphoreType.DMA((6,)),
            pltpu.SemaphoreType.DMA,
            pltpu.SemaphoreType.DMA((2,)),
            pltpu.SemaphoreType.DMA,
            pltpu.SemaphoreType.DMA((2,)),
        ],
        compiler_params=pltpu.CompilerParams(
            collective_id=0, has_side_effects=True, vmem_limit_bytes=48 * 2**20
        ),
        name="triangle",
    )(*[pltpu.with_memory_space_constraint(x, pltpu.HBM) for x in (pair, projection, out_weight)])


def solution(mesh):
    placed = (P("row", "col", None), P(), P())
    rows, cols = mesh.shape["row"], mesh.shape["col"]
    return jax.shard_map(
        functools.partial(local, rows, cols),
        mesh=mesh,
        in_specs=placed,
        out_specs=P("row", "col", None),
        check_vma=False,
    )
```

```python
import functools

import jax
import jax.numpy as jnp
from jax import lax
from jax.experimental import pallas as pl
from jax.experimental.pallas import tpu as pltpu
from jax.sharding import PartitionSpec as P

epsilon = 1e-05
MESH = pl.DeviceIdType.MESH
f32, bf16 = jnp.float32, jnp.bfloat16


def dot(a, b, dims):
    return lax.dot_general(a, b, (dims, ((), ())), preferred_element_type=f32)


def rem(a, b):
    return a % b if isinstance(a, int) else lax.rem(a, b)


def halves(first, second):
    return (
        jnp.concatenate([first[:, :64], second[:, :64]], axis=1),
        jnp.concatenate([first[:, 64:], second[:, 64:]], axis=1),
    )


def kernel(
    rows, cols, hidden,
    pair_hbm, projection_hbm, out_weight_hbm, update,
    pair, projection, out_weight, right_f32, left_f32, normed, gate, weights, right_send, left_send, right_got, left_got,
    right_all, left_all, mixed, mixed_send, mixed_got, mixed_f32,
    load_sem, entered_sem, send_sem, right_sem, left_sem, twin_sem, mixed_sem,
):
    chips = rows * cols // 2
    half_rows = rows // 2
    row, col = lax.axis_index("row"), lax.axis_index("col")
    planes, lines_z = rows // 4, 8
    columns = cols // 4
    x, y, z, core = col // 4, row // 4, rem(row, 4) * 2 + rem(col // 2, 2), rem(col, 2)
    half = row // half_rows
    slot_row = rem(row, half_rows)
    mine = row * (cols // 2) + col // 2
    twin = (row, col + 1 - 2 * core)

    def chip(x, y, z):
        return y * 4 + z // 2, x * 2 + rem(z, 2)

    def other(place, k, count):
        return rem(place + count // 2 + ((k + 1) // 2) * (1 - 2 * rem(k, 2)) + count, count)

    loads = [
        pltpu.make_async_copy(projection_hbm, projection, load_sem.at[0]),
        pltpu.make_async_copy(pair_hbm.at[pl.ds(0, 32)], pair.at[pl.ds(0, 32)], load_sem.at[1]),
        pltpu.make_async_copy(pair_hbm.at[pl.ds(32, 32)], pair.at[pl.ds(32, 32)], load_sem.at[2]),
        pltpu.make_async_copy(out_weight_hbm, out_weight, load_sem.at[3]),
    ]
    for load in loads:
        load.start()

    near = planes * lines_z
    barrier = pltpu.get_barrier_semaphore()
    x_peers = [(row, rem(col + 4 * step, cols)) for step in range(1, columns)]
    for k in range(lines_z):
        for step in range(planes // 2):
            other_y = core * (planes // 2) + other(rem(y, planes // 2), step, planes // 2)
            place, pair_place = chip(x, other_y, other(z, k, lines_z))
            peers = [(place, pair_place * 2 + 1 - core), (place, pair_place * 2 + core)]
            if k < lines_z - 1 or step < planes // 2 - 1:
                for peer in peers:
                    pl.semaphore_signal(barrier, inc=1, device_id=peer, device_id_type=MESH)
            else:
                pl.semaphore_signal(barrier, inc=1, device_id=peers[0], device_id_type=MESH)

                @pl.when(half != core)
                def _():
                    pl.semaphore_signal(barrier, inc=1, device_id=peers[1], device_id_type=MESH)

    for peer in [twin] + x_peers:
        pl.semaphore_signal(barrier, inc=1, device_id=peer, device_id_type=MESH)
    expected = near + columns - jnp.where(half == core, 1, 0)

    loads[0].wait()
    weights[...] = projection[:, : 4 * hidden].T

    def lines(step):
        block, inner = step // 8, rem(step, 8) * 2
        return block * 32 + inner

    def norm(step, _):
        top = lines(step)
        values = jnp.concatenate(
            [pair[top], pair[top + 16], pair[top + 1], pair[top + 17]], axis=0
        ).astype(f32)
        centered = values - jnp.mean(values, axis=-1, keepdims=True)
        variance = jnp.mean(centered * centered, axis=-1, keepdims=True)
        unit = (centered * lax.rsqrt(variance + epsilon)).astype(bf16)
        normed[step] = unit
        return 0

    def right_side(step, _):
        both = dot(weights[2 * hidden : 4 * hidden], normed[step], ((1,), (1,)))
        side = jax.nn.sigmoid(both[:hidden]) * both[hidden:]
        right_f32[pl.ds(2 * step, hidden, stride=32), :] = side[:, :128]
        right_f32[pl.ds(2 * step + 1, hidden, stride=32), :] = side[:, 128:]
        return 0

    def send_side(held, outgoing, got, sem, sent, first, stop, apart_too, with_own):
        def fill(channel):
            base = pl.multiple_of(channel * 32 + first, 16)
            outgoing[channel, first : first + 16] = held[pl.ds(base, 16), :].astype(bf16)
            return outgoing.at[channel, pl.ds(first, 16)]

        def body(step, _):
            apart = step // near
            place, pair_place = chip(
                other(x, apart, columns) if apart_too else x,
                other(y, rem(step // lines_z, planes), planes),
                other(z, rem(step, lines_z), lines_z),
            )
            pltpu.make_async_remote_copy(
                src_ref=fill(place * (cols // 2) + pair_place), dst_ref=got, send_sem=sent, recv_sem=sem,
                device_id=(place, pair_place * 2 + half), device_id_type=MESH,
            ).start()
            return 0

        own = stop - 1 if with_own else stop
        for step in range(0, own % 4):
            body(step, 0)
        lax.fori_loop(own % 4, own, body, 0, unroll=4)
        if with_own:
            source = fill(mine)

            @pl.when(half == core)
            def _():
                pltpu.make_async_copy(source, got, sem).start()

            @pl.when(half != core)
            def _():
                pltpu.make_async_remote_copy(
                    src_ref=source, dst_ref=got, send_sem=sent, recv_sem=sem, device_id=twin, device_id_type=MESH
                ).start()

    def send_right(part, stop, apart_too, with_own):
        got = right_got.at[half, col, slot_row, pl.ds(16 * part, 16)]
        send_side(right_f32, right_send, got, right_sem, send_sem.at[0], 16 * part, stop, apart_too, with_own)

    for part in range(2):
        loads[1 + part].wait()
        lax.fori_loop(8 * part, 8 * part + 8, norm, 0, unroll=2)
        lax.fori_loop(8 * part, 8 * part + 8, right_side, 0, unroll=4)
        if part == 0:
            pl.semaphore_wait(barrier, expected)
            for peer in x_peers:
                pl.semaphore_signal(entered_sem, inc=1, device_id=peer, device_id_type=MESH)
        send_right(part, near, False, True)
    pl.semaphore_wait(entered_sem, columns - 1)
    for part in range(2):
        send_right(part, chips - near, True, False)

    def left_side(step, _):
        both = dot(weights[: 2 * hidden], normed[step], ((1,), (1,)))
        side = jax.nn.sigmoid(both[:hidden]) * both[hidden:]
        left_f32[pl.ds(2 * step, hidden, stride=32), :] = side[:, :128]
        left_f32[pl.ds(2 * step + 1, hidden, stride=32), :] = side[:, 128:]
        return 0

    for part in range(2):
        lax.fori_loop(8 * part, 8 * part + 8, left_side, 0, unroll=4)
        send_side(
            left_f32, left_send, left_got.at[part, col, slot_row], left_sem.at[part], send_sem.at[1 + part],
            16 * part, chips, True, True,
        )

    def gate_of(step, _):
        gate[step] = jax.nn.sigmoid(dot(normed[step], projection[:, 4 * hidden :], ((1,), (0,))))
        return 0

    lax.fori_loop(0, 16, gate_of, 0, unroll=4)

    pltpu.make_async_copy(right_got.at[core], right_got.at[core], right_sem).wait()
    handed = pltpu.make_async_remote_copy(
        src_ref=right_got.at[core], dst_ref=right_got.at[core], send_sem=send_sem.at[3], recv_sem=twin_sem,
        device_id=twin, device_id_type=MESH,
    )
    handed.start()

    def arrange_right(which):
        def body(line, _):
            base = pl.multiple_of((which * half_rows + line) * 64, 64)
            for m in range(cols // 2):
                first, second = right_got[which, 2 * m, line], right_got[which, 2 * m + 1, line]
                low, high = halves(first, second)
                span = slice(128 * m, 128 * m + 128)
                right_all[pl.ds(base, 16), span] = low[:16]
                right_all[pl.ds(base + 16, 16), span] = high[:16]
                right_all[pl.ds(base + 32, 16), span] = low[16:]
                right_all[pl.ds(base + 48, 16), span] = high[16:]
            return 0

        lax.fori_loop(0, half_rows, body, 0)

    arrange_right(core)
    handed.wait_recv()
    arrange_right(1 - core)

    for part in range(2):
        pltpu.make_async_copy(left_got.at[part], left_got.at[part], left_sem.at[part]).wait()

        def arrange_left(line, _):
            base = pl.multiple_of(line * 32, 32)
            for m in range(cols // 2):
                low, high = halves(left_got[part, 2 * m, line], left_got[part, 2 * m + 1, line])
                left_all[pl.ds(base, 16), 128 * m : 128 * m + 128] = low
                left_all[pl.ds(base + 16, 16), 128 * m : 128 * m + 128] = high
            return 0

        lax.fori_loop(0, half_rows, arrange_left, 0)

        def multiply(step, _):
            base = pl.multiple_of(step * 256, 256)
            mixed[...] = dot(left_all[...], right_all[pl.ds(base, 256), :], ((1,), (1,))).astype(bf16)
            for line in range(half_rows):
                for m in range(2):
                    span = slice(128 * m, 128 * m + 128)
                    low, high = halves(mixed[line * 32 : line * 32 + 16, span], mixed[line * 32 + 16 : line * 32 + 32, span])
                    mixed_send[part, line, step * 4 + 2 * m] = low
                    mixed_send[part, line, step * 4 + 2 * m + 1] = high
            return 0

        lax.fori_loop(0, cols // 4, multiply, 0)

        got = mixed_got.at[part, mine]

        def mixed_message(place, to):
            line = rem(place, half_rows)
            return pltpu.make_async_remote_copy(
                src_ref=mixed_send.at[part, line, to], dst_ref=got,
                send_sem=send_sem.at[4 + part], recv_sem=mixed_sem.at[part],
                device_id=(place, to), device_id_type=MESH,
            )

        def send_mixed(step, _):
            other_core = other(core, rem(step // lines_z, 2), 2)
            other_y = core * (planes // 2) + other(rem(y, planes // 2), rem(step // (2 * lines_z), planes // 2), planes // 2)
            other_x = other(x, step // near, columns)
            place, pair_place = chip(other_x, other_y, other(z, rem(step, lines_z), lines_z))
            mixed_message(place, pair_place * 2 + other_core).start()
            return 0

        last = chips - 1
        for step in range(3):
            send_mixed(step, 0)
        lax.fori_loop(3, last, send_mixed, 0, unroll=4)
        place = core * half_rows + slot_row

        @pl.when(half == core)
        def _():
            pltpu.make_async_copy(mixed_send.at[part, slot_row, col], got, mixed_sem.at[part]).start()

        @pl.when(half != core)
        def _():
            mixed_message(place, col).start()

    loads[3].wait()
    for part in range(2):
        pltpu.make_async_copy(mixed_got.at[part], mixed_got.at[part], mixed_sem.at[part]).wait()

        total = jnp.zeros((16, 128), f32)
        total = lax.fori_loop(0, hidden, lambda c, t: t + mixed_got[part, c].astype(f32), total, unroll=min(32, hidden))
        mean = total * (1.0 / hidden)

        def square(c, t):
            centered = mixed_got[part, c].astype(f32) - mean
            return t + centered * centered

        scale = lax.rsqrt(lax.fori_loop(0, hidden, square, jnp.zeros((16, 128), f32), unroll=min(32, hidden)) * (1.0 / hidden) + epsilon)

        def scaled(c, _):
            mixed_f32[pl.ds(pl.multiple_of(c * 16, 16), 16), :] = (mixed_got[part, c].astype(f32) - mean) * scale
            return 0

        lax.fori_loop(0, hidden, scaled, 0, unroll=min(32, hidden))

        def finish(line, _):
            unit = mixed_f32[pl.ds(line, hidden, stride=16), :].astype(bf16)
            product = dot(unit, out_weight[...], ((0,), (0,)))
            step = part * 8 + line // 2
            result = (gate[step, pl.ds(pl.multiple_of(rem(line, 2) * 128, 128), 128), :] * product).astype(bf16)
            update[part * 32 + line] = result[:64]
            update[part * 32 + line + 16] = result[64:]
            return 0

        lax.fori_loop(0, 16, finish, 0, unroll=16)

    @pl.when(half == core)
    def _():
        pltpu.make_async_copy(right_send.at[pl.ds(0, chips - 1)], right_send.at[pl.ds(0, chips - 1)], send_sem.at[0]).wait()
        for part in range(2):
            span = left_send.at[pl.ds(0, chips - 1), pl.ds(0, 16)]
            pltpu.make_async_copy(span, span, send_sem.at[1 + part]).wait()
            span = mixed_got.at[0, pl.ds(0, chips - 1)]
            pltpu.make_async_copy(span, span, send_sem.at[4 + part]).wait()

    @pl.when(half != core)
    def _():
        pltpu.make_async_copy(right_send, right_send, send_sem.at[0]).wait()
        for part in range(2):
            span = left_send.at[:, pl.ds(0, 16)]
            pltpu.make_async_copy(span, span, send_sem.at[1 + part]).wait()
            span = mixed_got.at[0]
            pltpu.make_async_copy(span, span, send_sem.at[4 + part]).wait()

    handed.wait_send()


def local(rows, cols, pair, projection, out_weight):
    hidden = out_weight.shape[0]
    half_rows = rows // 2
    vmem = pl.BlockSpec(memory_space=pltpu.VMEM)
    length = cols * 64
    return pl.pallas_call(
        functools.partial(kernel, rows, cols, hidden),
        out_shape=jax.ShapeDtypeStruct(pair.shape, bf16),
        in_specs=[pl.BlockSpec(memory_space=pltpu.HBM)] * 3,
        out_specs=vmem,
        scratch_shapes=[
            pltpu.VMEM(pair.shape, bf16),
            pltpu.VMEM(projection.shape, bf16),
            pltpu.VMEM(out_weight.shape, bf16),
            pltpu.VMEM((hidden * 32, 128), f32),
            pltpu.VMEM((hidden * 32, 128), f32),
            pltpu.VMEM((16, 256, 128), bf16),
            pltpu.VMEM((16, 256, 128), f32),
            pltpu.VMEM((4 * hidden, 128), bf16),
            pltpu.VMEM((hidden, 32, 128), bf16),
            pltpu.VMEM((hidden, 32, 128), bf16),
            pltpu.VMEM((2, cols, half_rows, 32, 128), bf16),
            pltpu.VMEM((2, cols, half_rows, 16, 128), bf16),
            pltpu.VMEM((rows * 64, length), bf16),
            pltpu.VMEM((half_rows * 32, length), bf16),
            pltpu.VMEM((half_rows * 32, 256), bf16),
            pltpu.VMEM((2, half_rows, cols, 16, 128), bf16),
            pltpu.VMEM((2, hidden, 16, 128), bf16),
            pltpu.VMEM((hidden * 16, 128), f32),
            pltpu.SemaphoreType.DMA((4,)),
            pltpu.SemaphoreType.REGULAR,
            pltpu.SemaphoreType.DMA((6,)),
            pltpu.SemaphoreType.DMA,
            pltpu.SemaphoreType.DMA((2,)),
            pltpu.SemaphoreType.DMA,
            pltpu.SemaphoreType.DMA((2,)),
        ],
        compiler_params=pltpu.CompilerParams(
            collective_id=0, has_side_effects=True, vmem_limit_bytes=48 * 2**20
        ),
        name="triangle",
    )(*[pltpu.with_memory_space_constraint(x, pltpu.HBM) for x in (pair, projection, out_weight)])


def solution(mesh):
    placed = (P("row", "col", None), P(), P())
    rows, cols = mesh.shape["row"], mesh.shape["col"]
    return jax.shard_map(
        functools.partial(local, rows, cols),
        mesh=mesh,
        in_specs=placed,
        out_specs=P("row", "col", None),
        check_vma=False,
    )
```

```python
import functools

import jax
import jax.numpy as jnp
from jax import lax
from jax.experimental import pallas as pl
from jax.experimental.pallas import tpu as pltpu
from jax.sharding import PartitionSpec as P

epsilon = 1e-05
MESH = pl.DeviceIdType.MESH
f32, bf16 = jnp.float32, jnp.bfloat16


def dot(a, b, dims):
    return lax.dot_general(a, b, (dims, ((), ())), preferred_element_type=f32)


def rem(a, b):
    return a % b if isinstance(a, int) else lax.rem(a, b)


def halves(first, second):
    return (
        jnp.concatenate([first[:, :64], second[:, :64]], axis=1),
        jnp.concatenate([first[:, 64:], second[:, 64:]], axis=1),
    )


def kernel(
    rows, cols, hidden,
    pair_hbm, projection_hbm, out_weight_hbm, update,
    pair, projection, out_weight, right_f32, left_f32, normed, gate, weights, right_send, left_send, right_got, left_got,
    right_all, left_all, mixed, mixed_send, mixed_got, mixed_f32,
    load_sem, entered_sem, send_sem, right_sem, left_sem, twin_sem, mixed_sem,
):
    chips = rows * cols // 2
    half_rows = rows // 2
    row, col = lax.axis_index("row"), lax.axis_index("col")
    planes, lines_z = rows // 4, 8
    columns = cols // 4
    x, y, z, core = col // 4, row // 4, rem(row, 4) * 2 + rem(col // 2, 2), rem(col, 2)
    half = row // half_rows
    slot_row = rem(row, half_rows)
    mine = row * (cols // 2) + col // 2
    twin = (row, col + 1 - 2 * core)

    def chip(x, y, z):
        return y * 4 + z // 2, x * 2 + rem(z, 2)

    def other(place, k, count):
        return rem(place + count // 2 + ((k + 1) // 2) * (1 - 2 * rem(k, 2)) + count, count)

    loads = [
        pltpu.make_async_copy(projection_hbm, projection, load_sem.at[0]),
        pltpu.make_async_copy(pair_hbm.at[pl.ds(0, 32)], pair.at[pl.ds(0, 32)], load_sem.at[1]),
        pltpu.make_async_copy(pair_hbm.at[pl.ds(32, 32)], pair.at[pl.ds(32, 32)], load_sem.at[2]),
        pltpu.make_async_copy(out_weight_hbm, out_weight, load_sem.at[3]),
    ]
    for order in (1, 0, 2, 3):
        loads[order].start()

    near = planes * lines_z
    barrier = pltpu.get_barrier_semaphore()
    x_peers = [(row, rem(col + 4 * step, cols)) for step in range(1, columns)]
    for k in range(lines_z):
        for step in range(planes // 2):
            other_y = core * (planes // 2) + other(rem(y, planes // 2), step, planes // 2)
            place, pair_place = chip(x, other_y, other(z, k, lines_z))
            peers = [(place, pair_place * 2 + 1 - core), (place, pair_place * 2 + core)]
            if k < lines_z - 1 or step < planes // 2 - 1:
                for peer in peers:
                    pl.semaphore_signal(barrier, inc=1, device_id=peer, device_id_type=MESH)
            else:
                pl.semaphore_signal(barrier, inc=1, device_id=peers[0], device_id_type=MESH)

                @pl.when(half != core)
                def _():
                    pl.semaphore_signal(barrier, inc=1, device_id=peers[1], device_id_type=MESH)

    for peer in [twin] + x_peers:
        pl.semaphore_signal(barrier, inc=1, device_id=peer, device_id_type=MESH)
    expected = near + columns - jnp.where(half == core, 1, 0)

    def lines(step):
        block, inner = step // 8, rem(step, 8) * 2
        return block * 32 + inner

    def norm(step, _):
        top = lines(step)
        values = jnp.concatenate(
            [pair[top], pair[top + 16], pair[top + 1], pair[top + 17]], axis=0
        ).astype(f32)
        centered = values - jnp.mean(values, axis=-1, keepdims=True)
        variance = jnp.mean(centered * centered, axis=-1, keepdims=True)
        unit = (centered * lax.rsqrt(variance + epsilon)).astype(bf16)
        normed[step] = unit
        return 0

    def right_side(step, _):
        both = dot(weights[2 * hidden : 4 * hidden], normed[step], ((1,), (1,)))
        side = jax.nn.sigmoid(both[:hidden]) * both[hidden:]
        right_f32[pl.ds(2 * step, hidden, stride=32), :] = side[:, :128]
        right_f32[pl.ds(2 * step + 1, hidden, stride=32), :] = side[:, 128:]
        return 0

    def send_side(held, outgoing, got, sem, sent, first, stop, apart_too, with_own):
        def fill(channel):
            base = pl.multiple_of(channel * 32 + first, 16)
            outgoing[channel, first : first + 16] = held[pl.ds(base, 16), :].astype(bf16)
            return outgoing.at[channel, pl.ds(first, 16)]

        def body(step, _):
            apart = step // near
            place, pair_place = chip(
                other(x, apart, columns) if apart_too else x,
                other(y, rem(step // lines_z, planes), planes),
                other(z, rem(step, lines_z), lines_z),
            )
            pltpu.make_async_remote_copy(
                src_ref=fill(place * (cols // 2) + pair_place), dst_ref=got, send_sem=sent, recv_sem=sem,
                device_id=(place, pair_place * 2 + half), device_id_type=MESH,
            ).start()
            return 0

        own = stop - 1 if with_own else stop
        for step in range(0, own % 4):
            body(step, 0)
        lax.fori_loop(own % 4, own, body, 0, unroll=4)
        if with_own:
            source = fill(mine)

            @pl.when(half == core)
            def _():
                pltpu.make_async_copy(source, got, sem).start()

            @pl.when(half != core)
            def _():
                pltpu.make_async_remote_copy(
                    src_ref=source, dst_ref=got, send_sem=sent, recv_sem=sem, device_id=twin, device_id_type=MESH
                ).start()

    def send_right(part, stop, apart_too, with_own):
        got = right_got.at[half, col, slot_row, pl.ds(16 * part, 16)]
        send_side(right_f32, right_send, got, right_sem, send_sem.at[0], 16 * part, stop, apart_too, with_own)

    for part in range(2):
        loads[1 + part].wait()
        lax.fori_loop(8 * part, 8 * part + 8, norm, 0, unroll=2)
        if part == 0:
            loads[0].wait()
            weights[...] = projection[:, : 4 * hidden].T
        lax.fori_loop(8 * part, 8 * part + 8, right_side, 0, unroll=4)
        if part == 0:
            pl.semaphore_wait(barrier, expected)
            for peer in x_peers:
                pl.semaphore_signal(entered_sem, inc=1, device_id=peer, device_id_type=MESH)
        send_right(part, near, False, True)
    pl.semaphore_wait(entered_sem, columns - 1)
    for part in range(2):
        send_right(part, chips - near, True, False)

    def left_side(step, _):
        both = dot(weights[: 2 * hidden], normed[step], ((1,), (1,)))
        side = jax.nn.sigmoid(both[:hidden]) * both[hidden:]
        left_f32[pl.ds(2 * step, hidden, stride=32), :] = side[:, :128]
        left_f32[pl.ds(2 * step + 1, hidden, stride=32), :] = side[:, 128:]
        return 0

    for part in range(2):
        lax.fori_loop(8 * part, 8 * part + 8, left_side, 0, unroll=4)
        send_side(
            left_f32, left_send, left_got.at[part, col, slot_row], left_sem.at[part], send_sem.at[1 + part],
            16 * part, chips, True, True,
        )

    def gate_of(step, _):
        gate[step] = jax.nn.sigmoid(dot(normed[step], projection[:, 4 * hidden :], ((1,), (0,))))
        return 0

    lax.fori_loop(0, 16, gate_of, 0, unroll=4)

    pltpu.make_async_copy(right_got.at[core], right_got.at[core], right_sem).wait()
    handed = pltpu.make_async_remote_copy(
        src_ref=right_got.at[core], dst_ref=right_got.at[core], send_sem=send_sem.at[3], recv_sem=twin_sem,
        device_id=twin, device_id_type=MESH,
    )
    handed.start()

    def arrange_right(which):
        def body(line, _):
            base = pl.multiple_of((which * half_rows + line) * 64, 64)
            for m in range(cols // 2):
                first, second = right_got[which, 2 * m, line], right_got[which, 2 * m + 1, line]
                low, high = halves(first, second)
                span = slice(128 * m, 128 * m + 128)
                right_all[pl.ds(base, 16), span] = low[:16]
                right_all[pl.ds(base + 16, 16), span] = high[:16]
                right_all[pl.ds(base + 32, 16), span] = low[16:]
                right_all[pl.ds(base + 48, 16), span] = high[16:]
            return 0

        lax.fori_loop(0, half_rows, body, 0)

    arrange_right(core)
    handed.wait_recv()
    arrange_right(1 - core)

    for part in range(2):
        pltpu.make_async_copy(left_got.at[part], left_got.at[part], left_sem.at[part]).wait()

        def arrange_left(line, _):
            base = pl.multiple_of(line * 32, 32)
            for m in range(cols // 2):
                low, high = halves(left_got[part, 2 * m, line], left_got[part, 2 * m + 1, line])
                left_all[pl.ds(base, 16), 128 * m : 128 * m + 128] = low
                left_all[pl.ds(base + 16, 16), 128 * m : 128 * m + 128] = high
            return 0

        lax.fori_loop(0, half_rows, arrange_left, 0)

        def multiply(step, _):
            base = pl.multiple_of(step * 256, 256)
            mixed[...] = dot(left_all[...], right_all[pl.ds(base, 256), :], ((1,), (1,))).astype(bf16)
            for line in range(half_rows):
                for m in range(2):
                    span = slice(128 * m, 128 * m + 128)
                    low, high = halves(mixed[line * 32 : line * 32 + 16, span], mixed[line * 32 + 16 : line * 32 + 32, span])
                    mixed_send[part, line, step * 4 + 2 * m] = low
                    mixed_send[part, line, step * 4 + 2 * m + 1] = high
            return 0

        lax.fori_loop(0, cols // 4, multiply, 0)

        got = mixed_got.at[part, mine]

        def mixed_message(place, to):
            line = rem(place, half_rows)
            return pltpu.make_async_remote_copy(
                src_ref=mixed_send.at[part, line, to], dst_ref=got,
                send_sem=send_sem.at[4 + part], recv_sem=mixed_sem.at[part],
                device_id=(place, to), device_id_type=MESH,
            )

        def send_mixed(step, _):
            other_core = other(core, rem(step // lines_z, 2), 2)
            other_y = core * (planes // 2) + other(rem(y, planes // 2), rem(step // (2 * lines_z), planes // 2), planes // 2)
            other_x = other(x, step // near, columns)
            place, pair_place = chip(other_x, other_y, other(z, rem(step, lines_z), lines_z))
            mixed_message(place, pair_place * 2 + other_core).start()
            return 0

        last = chips - 1
        for step in range(3):
            send_mixed(step, 0)
        lax.fori_loop(3, last, send_mixed, 0, unroll=4)
        place = core * half_rows + slot_row

        @pl.when(half == core)
        def _():
            pltpu.make_async_copy(mixed_send.at[part, slot_row, col], got, mixed_sem.at[part]).start()

        @pl.when(half != core)
        def _():
            mixed_message(place, col).start()

    loads[3].wait()
    for part in range(2):
        pltpu.make_async_copy(mixed_got.at[part], mixed_got.at[part], mixed_sem.at[part]).wait()

        total = jnp.zeros((16, 128), f32)
        total = lax.fori_loop(0, hidden, lambda c, t: t + mixed_got[part, c].astype(f32), total, unroll=min(32, hidden))
        mean = total * (1.0 / hidden)

        def square(c, t):
            centered = mixed_got[part, c].astype(f32) - mean
            return t + centered * centered

        scale = lax.rsqrt(lax.fori_loop(0, hidden, square, jnp.zeros((16, 128), f32), unroll=min(32, hidden)) * (1.0 / hidden) + epsilon)

        def scaled(c, _):
            mixed_f32[pl.ds(pl.multiple_of(c * 16, 16), 16), :] = (mixed_got[part, c].astype(f32) - mean) * scale
            return 0

        lax.fori_loop(0, hidden, scaled, 0, unroll=min(32, hidden))

        def finish(line, _):
            unit = mixed_f32[pl.ds(line, hidden, stride=16), :].astype(bf16)
            product = dot(unit, out_weight[...], ((0,), (0,)))
            step = part * 8 + line // 2
            result = (gate[step, pl.ds(pl.multiple_of(rem(line, 2) * 128, 128), 128), :] * product).astype(bf16)
            update[part * 32 + line] = result[:64]
            update[part * 32 + line + 16] = result[64:]
            return 0

        lax.fori_loop(0, 16, finish, 0, unroll=16)

    @pl.when(half == core)
    def _():
        pltpu.make_async_copy(right_send.at[pl.ds(0, chips - 1)], right_send.at[pl.ds(0, chips - 1)], send_sem.at[0]).wait()
        for part in range(2):
            span = left_send.at[pl.ds(0, chips - 1), pl.ds(0, 16)]
            pltpu.make_async_copy(span, span, send_sem.at[1 + part]).wait()
            span = mixed_got.at[0, pl.ds(0, chips - 1)]
            pltpu.make_async_copy(span, span, send_sem.at[4 + part]).wait()

    @pl.when(half != core)
    def _():
        pltpu.make_async_copy(right_send, right_send, send_sem.at[0]).wait()
        for part in range(2):
            span = left_send.at[:, pl.ds(0, 16)]
            pltpu.make_async_copy(span, span, send_sem.at[1 + part]).wait()
            span = mixed_got.at[0]
            pltpu.make_async_copy(span, span, send_sem.at[4 + part]).wait()

    handed.wait_send()


def local(rows, cols, pair, projection, out_weight):
    hidden = out_weight.shape[0]
    half_rows = rows // 2
    vmem = pl.BlockSpec(memory_space=pltpu.VMEM)
    length = cols * 64
    return pl.pallas_call(
        functools.partial(kernel, rows, cols, hidden),
        out_shape=jax.ShapeDtypeStruct(pair.shape, bf16),
        in_specs=[pl.BlockSpec(memory_space=pltpu.HBM)] * 3,
        out_specs=vmem,
        scratch_shapes=[
            pltpu.VMEM(pair.shape, bf16),
            pltpu.VMEM(projection.shape, bf16),
            pltpu.VMEM(out_weight.shape, bf16),
            pltpu.VMEM((hidden * 32 + 32, 128), f32),
            pltpu.VMEM((hidden * 32 + 32, 128), f32),
            pltpu.VMEM((16, 256, 128), bf16),
            pltpu.VMEM((16, 256, 128), f32),
            pltpu.VMEM((4 * hidden, 128), bf16),
            pltpu.VMEM((hidden, 32, 128), bf16),
            pltpu.VMEM((hidden, 32, 128), bf16),
            pltpu.VMEM((2, cols, half_rows, 32, 128), bf16),
            pltpu.VMEM((2, cols, half_rows, 16, 128), bf16),
            pltpu.VMEM((rows * 64, length), bf16),
            pltpu.VMEM((half_rows * 32, length), bf16),
            pltpu.VMEM((half_rows * 32, 256), bf16),
            pltpu.VMEM((2, half_rows, cols, 16, 128), bf16),
            pltpu.VMEM((2, hidden, 16, 128), bf16),
            pltpu.VMEM((hidden * 16 + 16, 128), f32),
            pltpu.SemaphoreType.DMA((4,)),
            pltpu.SemaphoreType.REGULAR,
            pltpu.SemaphoreType.DMA((6,)),
            pltpu.SemaphoreType.DMA,
            pltpu.SemaphoreType.DMA((2,)),
            pltpu.SemaphoreType.DMA,
            pltpu.SemaphoreType.DMA((2,)),
        ],
        compiler_params=pltpu.CompilerParams(
            collective_id=0, has_side_effects=True, vmem_limit_bytes=48 * 2**20
        ),
        name="triangle",
    )(*[pltpu.with_memory_space_constraint(x, pltpu.HBM) for x in (pair, projection, out_weight)])


def solution(mesh):
    placed = (P("row", "col", None), P(), P())
    rows, cols = mesh.shape["row"], mesh.shape["col"]
    return jax.shard_map(
        functools.partial(local, rows, cols),
        mesh=mesh,
        in_specs=placed,
        out_specs=P("row", "col", None),
        check_vma=False,
    )
```

```python
import functools

import jax
import jax.numpy as jnp
from jax import lax
from jax.experimental import pallas as pl
from jax.experimental.pallas import tpu as pltpu
from jax.sharding import PartitionSpec as P

epsilon = 1e-05
MESH = pl.DeviceIdType.MESH
f32, bf16 = jnp.float32, jnp.bfloat16


def dot(a, b, dims):
    return lax.dot_general(a, b, (dims, ((), ())), preferred_element_type=f32)


def rem(a, b):
    return a % b if isinstance(a, int) else lax.rem(a, b)


def halves(first, second):
    return (
        jnp.concatenate([first[:, :64], second[:, :64]], axis=1),
        jnp.concatenate([first[:, 64:], second[:, 64:]], axis=1),
    )


def kernel(
    rows, cols, hidden,
    pair_hbm, projection_hbm, out_weight_hbm, update,
    pair, projection, out_weight, right_f32, left_f32, normed, gate, weights, right_send, left_send, right_got, left_got,
    right_all, left_all, mixed, mixed_send, mixed_got, mixed_f32,
    load_sem, entered_sem, send_sem, right_sem, left_sem, twin_sem, mixed_sem,
):
    chips = rows * cols // 2
    half_rows = rows // 2
    row, col = lax.axis_index("row"), lax.axis_index("col")
    planes, lines_z = rows // 4, 8
    columns = cols // 4
    x, y, z, core = col // 4, row // 4, rem(row, 4) * 2 + rem(col // 2, 2), rem(col, 2)
    half = row // half_rows
    slot_row = rem(row, half_rows)
    mine = row * (cols // 2) + col // 2
    twin = (row, col + 1 - 2 * core)

    def chip(x, y, z):
        return y * 4 + z // 2, x * 2 + rem(z, 2)

    def other(place, k, count):
        return rem(place + count // 2 + ((k + 1) // 2) * (1 - 2 * rem(k, 2)) + count, count)

    loads = [
        pltpu.make_async_copy(projection_hbm, projection, load_sem.at[0]),
        pltpu.make_async_copy(pair_hbm.at[pl.ds(0, 32)], pair.at[pl.ds(0, 32)], load_sem.at[1]),
        pltpu.make_async_copy(pair_hbm.at[pl.ds(32, 32)], pair.at[pl.ds(32, 32)], load_sem.at[2]),
        pltpu.make_async_copy(out_weight_hbm, out_weight, load_sem.at[3]),
    ]
    for order in (1, 0, 2, 3):
        loads[order].start()

    near = planes * lines_z
    barrier = pltpu.get_barrier_semaphore()
    x_peers = [(row, rem(col + 4 * step, cols)) for step in range(1, columns)]
    for k in range(lines_z):
        for step in range(planes // 2):
            other_y = core * (planes // 2) + other(rem(y, planes // 2), step, planes // 2)
            place, pair_place = chip(x, other_y, other(z, k, lines_z))
            peers = [(place, pair_place * 2 + 1 - core), (place, pair_place * 2 + core)]
            if k < lines_z - 1 or step < planes // 2 - 1:
                for peer in peers:
                    pl.semaphore_signal(barrier, inc=1, device_id=peer, device_id_type=MESH)
            else:
                pl.semaphore_signal(barrier, inc=1, device_id=peers[0], device_id_type=MESH)

                @pl.when(half != core)
                def _():
                    pl.semaphore_signal(barrier, inc=1, device_id=peers[1], device_id_type=MESH)

    for peer in [twin] + x_peers:
        pl.semaphore_signal(barrier, inc=1, device_id=peer, device_id_type=MESH)
    expected = near + columns - jnp.where(half == core, 1, 0)

    def lines(step):
        block, inner = step // 8, rem(step, 8) * 2
        return block * 32 + inner

    def norm(step, _):
        top = lines(step)
        values = jnp.concatenate(
            [pair[top], pair[top + 16], pair[top + 1], pair[top + 17]], axis=0
        ).astype(f32)
        centered = values - jnp.mean(values, axis=-1, keepdims=True)
        variance = jnp.mean(centered * centered, axis=-1, keepdims=True)
        unit = (centered * lax.rsqrt(variance + epsilon)).astype(bf16)
        normed[step] = unit
        return 0

    def right_side(step, _):
        both = dot(weights[2 * hidden : 4 * hidden], normed[step], ((1,), (1,)))
        side = jax.nn.sigmoid(both[:hidden]) * both[hidden:]
        right_f32[pl.ds(2 * step, hidden, stride=32), :] = side[:, :128]
        right_f32[pl.ds(2 * step + 1, hidden, stride=32), :] = side[:, 128:]
        return 0

    def send_side(held, outgoing, got, sem, sent, first, stop, apart_too, with_own):
        def fill(channel):
            base = pl.multiple_of(channel * 32 + first, 16)
            outgoing[channel, first : first + 16] = held[pl.ds(base, 16), :].astype(bf16)
            return outgoing.at[channel, pl.ds(first, 16)]

        def body(step, _):
            apart = step // near
            place, pair_place = chip(
                other(x, apart, columns) if apart_too else x,
                other(y, rem(step // lines_z, planes), planes),
                other(z, rem(step, lines_z), lines_z),
            )
            pltpu.make_async_remote_copy(
                src_ref=fill(place * (cols // 2) + pair_place), dst_ref=got, send_sem=sent, recv_sem=sem,
                device_id=(place, pair_place * 2 + half), device_id_type=MESH,
            ).start()
            return 0

        own = stop - 1 if with_own else stop
        for step in range(0, own % 4):
            body(step, 0)
        lax.fori_loop(own % 4, own, body, 0, unroll=4)
        if with_own:
            source = fill(mine)

            @pl.when(half == core)
            def _():
                pltpu.make_async_copy(source, got, sem).start()

            @pl.when(half != core)
            def _():
                pltpu.make_async_remote_copy(
                    src_ref=source, dst_ref=got, send_sem=sent, recv_sem=sem, device_id=twin, device_id_type=MESH
                ).start()

    def send_right(part, stop, apart_too, with_own):
        got = right_got.at[half, col, slot_row, pl.ds(16 * part, 16)]
        send_side(right_f32, right_send, got, right_sem, send_sem.at[0], 16 * part, stop, apart_too, with_own)

    for part in range(2):
        loads[1 + part].wait()
        lax.fori_loop(8 * part, 8 * part + 8, norm, 0, unroll=2)
        if part == 0:
            loads[0].wait()
            weights[...] = projection[:, : 4 * hidden].T
        lax.fori_loop(8 * part, 8 * part + 8, right_side, 0, unroll=4)
        if part == 0:
            pl.semaphore_wait(barrier, expected)
            for peer in x_peers:
                pl.semaphore_signal(entered_sem, inc=1, device_id=peer, device_id_type=MESH)
        send_right(part, near, False, True)
    pl.semaphore_wait(entered_sem, columns - 1)
    for part in range(2):
        send_right(part, chips - near, True, False)

    def left_side(step, _):
        both = dot(weights[: 2 * hidden], normed[step], ((1,), (1,)))
        side = jax.nn.sigmoid(both[:hidden]) * both[hidden:]
        left_f32[pl.ds(2 * step, hidden, stride=32), :] = side[:, :128]
        left_f32[pl.ds(2 * step + 1, hidden, stride=32), :] = side[:, 128:]
        return 0

    for part in range(2):
        lax.fori_loop(8 * part, 8 * part + 8, left_side, 0, unroll=4)
        send_side(
            left_f32, left_send, left_got.at[part, col, slot_row], left_sem.at[part], send_sem.at[1 + part],
            16 * part, chips, True, True,
        )

    def gate_of(step, _):
        gate[step] = jax.nn.sigmoid(dot(normed[step], projection[:, 4 * hidden :], ((1,), (0,))))
        return 0

    lax.fori_loop(0, 16, gate_of, 0, unroll=4)

    pltpu.make_async_copy(right_got.at[core], right_got.at[core], right_sem).wait()
    handed = pltpu.make_async_remote_copy(
        src_ref=right_got.at[core], dst_ref=right_got.at[core], send_sem=send_sem.at[3], recv_sem=twin_sem,
        device_id=twin, device_id_type=MESH,
    )
    handed.start()

    def arrange_right(which):
        def body(line, _):
            base = pl.multiple_of((which * half_rows + line) * 64, 64)
            for m in range(cols // 2):
                first, second = right_got[which, 2 * m, line], right_got[which, 2 * m + 1, line]
                low, high = halves(first, second)
                span = slice(128 * m, 128 * m + 128)
                right_all[pl.ds(base, 16), span] = low[:16]
                right_all[pl.ds(base + 16, 16), span] = high[:16]
                right_all[pl.ds(base + 32, 16), span] = low[16:]
                right_all[pl.ds(base + 48, 16), span] = high[16:]
            return 0

        lax.fori_loop(0, half_rows, body, 0)

    arrange_right(core)
    handed.wait_recv()
    arrange_right(1 - core)

    for part in range(2):
        pltpu.make_async_copy(left_got.at[part], left_got.at[part], left_sem.at[part]).wait()

        def arrange_left(line, _):
            base = pl.multiple_of(line * 32, 32)
            for m in range(cols // 2):
                low, high = halves(left_got[part, 2 * m, line], left_got[part, 2 * m + 1, line])
                left_all[pl.ds(base, 16), 128 * m : 128 * m + 128] = low
                left_all[pl.ds(base + 16, 16), 128 * m : 128 * m + 128] = high
            return 0

        lax.fori_loop(0, half_rows, arrange_left, 0)

        def multiply(step, _):
            base = pl.multiple_of(step * 256, 256)
            mixed[...] = dot(left_all[...], right_all[pl.ds(base, 256), :], ((1,), (1,))).astype(bf16)
            for line in range(half_rows):
                for m in range(2):
                    span = slice(128 * m, 128 * m + 128)
                    low, high = halves(mixed[line * 32 : line * 32 + 16, span], mixed[line * 32 + 16 : line * 32 + 32, span])
                    mixed_send[part, line, step * 4 + 2 * m] = low
                    mixed_send[part, line, step * 4 + 2 * m + 1] = high
            return 0

        lax.fori_loop(0, cols // 4, multiply, 0)

        got = mixed_got.at[part, mine]

        def mixed_message(place, to):
            line = rem(place, half_rows)
            return pltpu.make_async_remote_copy(
                src_ref=mixed_send.at[part, line, to], dst_ref=got,
                send_sem=send_sem.at[4 + part], recv_sem=mixed_sem.at[part],
                device_id=(place, to), device_id_type=MESH,
            )

        def send_mixed(step, _):
            other_core = other(core, rem(step // lines_z, 2), 2)
            other_y = core * (planes // 2) + other(rem(y, planes // 2), rem(step // (2 * lines_z), planes // 2), planes // 2)
            other_x = other(x, step // near, columns)
            place, pair_place = chip(other_x, other_y, other(z, rem(step, lines_z), lines_z))
            mixed_message(place, pair_place * 2 + other_core).start()
            return 0

        last = chips - 1
        for step in range(3):
            send_mixed(step, 0)
        lax.fori_loop(3, last, send_mixed, 0, unroll=4)
        place = core * half_rows + slot_row

        @pl.when(half == core)
        def _():
            pltpu.make_async_copy(mixed_send.at[part, slot_row, col], got, mixed_sem.at[part]).start()

        @pl.when(half != core)
        def _():
            mixed_message(place, col).start()

    loads[3].wait()
    for part in range(2):
        pltpu.make_async_copy(mixed_got.at[part], mixed_got.at[part], mixed_sem.at[part]).wait()

        def sum_of(term):
            zero = jnp.zeros((16, 128), f32)
            sums = lax.fori_loop(
                0, hidden // 4, lambda c, t: tuple(t[n] + term(4 * c + n) for n in range(4)), (zero,) * 4, unroll=8
            )
            return (sums[0] + sums[1]) + (sums[2] + sums[3])

        mean = sum_of(lambda c: mixed_got[part, c].astype(f32)) * (1.0 / hidden)

        def square(c):
            centered = mixed_got[part, c].astype(f32) - mean
            return centered * centered

        scale = lax.rsqrt(sum_of(square) * (1.0 / hidden) + epsilon)

        def scaled(c, _):
            mixed_f32[pl.ds(pl.multiple_of(c * 16, 16), 16), :] = (mixed_got[part, c].astype(f32) - mean) * scale
            return 0

        lax.fori_loop(0, hidden, scaled, 0, unroll=min(32, hidden))

        def finish(line, _):
            unit = mixed_f32[pl.ds(line, hidden, stride=16), :].astype(bf16)
            product = dot(unit, out_weight[...], ((0,), (0,)))
            step = part * 8 + line // 2
            result = (gate[step, pl.ds(pl.multiple_of(rem(line, 2) * 128, 128), 128), :] * product).astype(bf16)
            update[part * 32 + line] = result[:64]
            update[part * 32 + line + 16] = result[64:]
            return 0

        lax.fori_loop(0, 16, finish, 0, unroll=16)

    @pl.when(half == core)
    def _():
        pltpu.make_async_copy(right_send.at[pl.ds(0, chips - 1)], right_send.at[pl.ds(0, chips - 1)], send_sem.at[0]).wait()
        for part in range(2):
            span = left_send.at[pl.ds(0, chips - 1), pl.ds(0, 16)]
            pltpu.make_async_copy(span, span, send_sem.at[1 + part]).wait()
            span = mixed_got.at[0, pl.ds(0, chips - 1)]
            pltpu.make_async_copy(span, span, send_sem.at[4 + part]).wait()

    @pl.when(half != core)
    def _():
        pltpu.make_async_copy(right_send, right_send, send_sem.at[0]).wait()
        for part in range(2):
            span = left_send.at[:, pl.ds(0, 16)]
            pltpu.make_async_copy(span, span, send_sem.at[1 + part]).wait()
            span = mixed_got.at[0]
            pltpu.make_async_copy(span, span, send_sem.at[4 + part]).wait()

    handed.wait_send()


def local(rows, cols, pair, projection, out_weight):
    hidden = out_weight.shape[0]
    half_rows = rows // 2
    vmem = pl.BlockSpec(memory_space=pltpu.VMEM)
    length = cols * 64
    return pl.pallas_call(
        functools.partial(kernel, rows, cols, hidden),
        out_shape=jax.ShapeDtypeStruct(pair.shape, bf16),
        in_specs=[pl.BlockSpec(memory_space=pltpu.HBM)] * 3,
        out_specs=vmem,
        scratch_shapes=[
            pltpu.VMEM(pair.shape, bf16),
            pltpu.VMEM(projection.shape, bf16),
            pltpu.VMEM(out_weight.shape, bf16),
            pltpu.VMEM((hidden * 32 + 32, 128), f32),
            pltpu.VMEM((hidden * 32 + 32, 128), f32),
            pltpu.VMEM((16, 256, 128), bf16),
            pltpu.VMEM((16, 256, 128), f32),
            pltpu.VMEM((4 * hidden, 128), bf16),
            pltpu.VMEM((hidden, 32, 128), bf16),
            pltpu.VMEM((hidden, 32, 128), bf16),
            pltpu.VMEM((2, cols, half_rows, 32, 128), bf16),
            pltpu.VMEM((2, cols, half_rows, 16, 128), bf16),
            pltpu.VMEM((rows * 64, length), bf16),
            pltpu.VMEM((half_rows * 32, length), bf16),
            pltpu.VMEM((half_rows * 32, 256), bf16),
            pltpu.VMEM((2, half_rows, cols, 16, 128), bf16),
            pltpu.VMEM((2, hidden, 16, 128), bf16),
            pltpu.VMEM((hidden * 16 + 16, 128), f32),
            pltpu.SemaphoreType.DMA((4,)),
            pltpu.SemaphoreType.REGULAR,
            pltpu.SemaphoreType.DMA((6,)),
            pltpu.SemaphoreType.DMA,
            pltpu.SemaphoreType.DMA((2,)),
            pltpu.SemaphoreType.DMA,
            pltpu.SemaphoreType.DMA((2,)),
        ],
        compiler_params=pltpu.CompilerParams(
            collective_id=0, has_side_effects=True, vmem_limit_bytes=48 * 2**20
        ),
        name="triangle",
    )(*[pltpu.with_memory_space_constraint(x, pltpu.HBM) for x in (pair, projection, out_weight)])


def solution(mesh):
    placed = (P("row", "col", None), P(), P())
    rows, cols = mesh.shape["row"], mesh.shape["col"]
    return jax.shard_map(
        functools.partial(local, rows, cols),
        mesh=mesh,
        in_specs=placed,
        out_specs=P("row", "col", None),
        check_vma=False,
    )
```
